128 devices in a mesh: lvl: 8 (over y, core), clu: 16 (over z, x).
Axes of the slice: x: 4, y: 4, z: 4, core: 2. Of those that a mesh axis runs over, the one named last changes fastest.
Arguments:
- sources: bfloat16 [32, 2, 2097152], P(None, None, ('lvl', 'clu')), may hold values from -6 to 6
- source_order: int32 [128, 16384], P(('lvl', 'clu')), may hold values from 0 to 16383, each once within a row
- leaf_basis: bfloat16 [8192, 256, 128], P(('lvl', 'clu')), may hold values from -0.25 to 0.25
- leaf_ranks: int32 [8192], P(('lvl', 'clu')), may hold values from 16 to 64, as said below
- source_factors: bfloat16 [3, 8192, 2, 64, 128], P(None, ('lvl', 'clu')), may hold values from -0.375 to 0.375
- target_factors: bfloat16 [4, 8192, 2, 64, 128], P(None, ('lvl', 'clu')), may hold values from -0.375 to 0.375
- target_basis: bfloat16 [8192, 64, 512], P(('lvl', 'clu')), may hold values from -0.5 to 0.5
- target_order: int32 [128, 16384], P(('lvl', 'clu')), may hold values from 0 to 16383, each once within a row
Outputs:
- fields: bfloat16 [32, 2, 2097152], P(None, None, ('lvl', 'clu'))
The draws below stay inside these ranges and needn't reach their ends.
Inputs may be any that keep to these rules, and one draw needn't show every extreme that they name: `leaf_ranks`: some leaf has rank 64.
All inputs are finite; a program needn't handle non-finite values.
Results may differ from the reference program's by a relative error of at most 0.019.
Values may be sent and summed in bfloat16 or wider, within the bound.
No kernel may reach another device: no remote copies, remote signals or barrier semaphores. Data moves between devices by JAX's collectives and lax.ppermute only.
A program may use at most 128 MiB of HBM per device.

```python
import jax
import jax.numpy as jnp

R = 64
NRHS = 32
B = 256
LOW = 4
M = 64
P_SIZE = 8192
NSRC = 2097152
NTGT = 2097152
LVL_BITS = 3
CLU_BITS = 4
N_LVL = 8
N_CLU = 16


def draw_leaf_ranks(key, part):
    key = jax.random.fold_in(key, 3)
    values = jax.random.randint(key, (P_SIZE,), R // 4, R + 1, dtype=jnp.int32)
    return values.at[0].set(R)


def shard_levels(key, dims, shards, low, high):
    gain = 1.0
    for axis_at, blocks in shards:
        steps = jax.random.uniform(jax.random.fold_in(jax.random.fold_in(key, 6), axis_at), (blocks,), jnp.float32, low / len(shards), high / len(shards))
        gain = gain * jnp.repeat(jnp.exp(steps), dims[axis_at] // blocks).reshape((-1,) + (1,) * (len(dims) - 1 - axis_at))
    return gain


def gaussian(rng, extent, scale, limit, cuts=(), kind=jnp.bfloat16):
    entries = jax.random.normal(rng, extent, jnp.float32) * scale
    if len(cuts) > 0:
        entries = shard_levels(rng, extent, cuts, -0.22, 0.18) * entries
    return jnp.clip(entries, min=-limit, max=limit).astype(kind)


def setup_inputs(seed: int = 0) -> dict:
    keys = jax.random.split(jax.random.key(seed), 9)
    return {
        "sources": gaussian(keys[0], (NRHS, 2, NSRC), 1.0, 6.0, ((2, 128),)),
        "source_order": jax.vmap(lambda own: jax.random.permutation(own, M * B))(jax.random.split(keys[1], (N_LVL * N_CLU))).reshape((N_LVL * N_CLU, M * B)).astype(jnp.int32),
        "leaf_basis": gaussian(keys[2], (P_SIZE, B, 2 * R), (2 * B) ** -0.5, 0.25, ((0, 128),)),
        "leaf_ranks": draw_leaf_ranks(jax.random.fold_in(keys[8], 71), 0),
        "source_factors": gaussian(keys[4], (LVL_BITS, P_SIZE, 2, R, 2 * R), (4 * R) ** -0.5, 0.375, ((1, 128),)),
        "target_factors": gaussian(keys[5], (CLU_BITS, P_SIZE, 2, R, 2 * R), (4 * R) ** -0.5, 0.375, ((1, 128),)),
        "target_basis": gaussian(keys[6], (P_SIZE, R, 2 * B), (2 * R) ** -0.5, 0.5, ((0, 128),)),
        "target_order": jax.vmap(lambda own: jax.random.permutation(own, M * B))(jax.random.split(keys[7], (N_LVL * N_CLU))).reshape((N_LVL * N_CLU, M * B)).astype(jnp.int32),
    }


def expand(matrix):
    half_width = matrix.shape[-1] // 2
    rotated = jnp.concatenate([-matrix[..., half_width:], matrix[..., :half_width]], axis=-1)
    return jnp.concatenate([matrix, rotated], axis=-2)


def combine_pair(low_side, higher, factor):
    front = expand(factor[..., 0, :, :].astype(jnp.float32))
    back = expand(factor[..., 1, :, :].astype(jnp.float32))
    return (jnp.einsum('...rk,...kl->...rl', low_side.astype(jnp.float32), front)
            + jnp.einsum('...rk,...kl->...rl', higher.astype(jnp.float32), back))


def apply_level(coeffs, factors, stride):
    total_pairs = coeffs.shape[0]
    blocks = total_pairs // (2 * stride)
    grouped = coeffs.reshape((blocks, 2, stride) + coeffs.shape[1:])
    weights = factors.reshape((blocks, 2, stride) + factors.shape[1:])
    low_side = grouped[:, 0]
    higher = grouped[:, 1]
    mixed = jnp.stack([combine_pair(low_side, higher, weights[:, 0]),
                       combine_pair(low_side, higher, weights[:, 1])], axis=1)
    return mixed.reshape(coeffs.shape).astype(jnp.bfloat16)


def reference(sources, source_order, leaf_basis, leaf_ranks, source_factors, target_factors, target_basis, target_order):
    devices = N_LVL * N_CLU
    per_dev = M * B
    grouped = sources.reshape(NRHS, 2, devices, per_dev)
    index_src = jnp.broadcast_to(source_order[None, None, :, :], grouped.shape)
    clustered = jnp.take_along_axis(grouped, index_src, axis=3).reshape(NRHS, 2, P_SIZE, B).astype(jnp.float32)
    basis = leaf_basis.astype(jnp.float32)
    rotated = jnp.concatenate([-basis[..., R:], basis[..., :R]], axis=-1)
    leaf_coef = (jnp.einsum('rpb,pbk->prk', clustered[:, 0], basis)
                 + jnp.einsum('rpb,pbk->prk', clustered[:, 1], rotated))
    inside = (jnp.arange(2 * R) % R)[None, :] < leaf_ranks[:, None]
    coeffs = jnp.where(inside[:, None, :], leaf_coef, 0.0).astype(jnp.bfloat16)
    for bit_index in range(LVL_BITS):
        coeffs = apply_level(coeffs, source_factors[bit_index], (2 ** bit_index) * N_CLU * M)
    coeffs = coeffs.reshape(N_LVL, N_CLU, N_CLU, LOW, NRHS, 2 * R)
    coeffs = coeffs.transpose(0, 2, 1, 3, 4, 5).reshape(P_SIZE, NRHS, 2 * R)
    for bit_index in range(CLU_BITS):
        coeffs = apply_level(coeffs, target_factors[bit_index], (2 ** bit_index) * LOW)
    expansion = expand(target_basis.astype(jnp.float32))
    target_field = jnp.einsum('prk,pkq->prq', coeffs.astype(jnp.float32), expansion)
    target_field = target_field.reshape(devices, M, NRHS, 2, B).transpose(2, 3, 0, 1, 4).reshape(NRHS, 2, devices, per_dev)
    index_tgt = jnp.broadcast_to(target_order[None, None, :, :], target_field.shape)
    placed = jnp.take_along_axis(target_field, index_tgt, axis=3)
    return placed.reshape(NRHS, 2, NTGT).astype(jnp.bfloat16)
```

```python
import functools

import jax
import jax.numpy as jnp
from jax import lax
from jax.experimental import pallas as pl
from jax.experimental.pallas import tpu as pltpu
from jax.sharding import PartitionSpec as P

F32 = jnp.float32
BF16 = jnp.bfloat16
LANES = 128
CUTS = ((0, 4),)


def lane_halves(shape):
    return lax.broadcasted_iota(jnp.int32, shape, 1) < shape[1] // 2


def packed_sum(first, second):
    turned = pltpu.roll(second, second.shape[1] // 2, 1)
    return first + jnp.where(lane_halves(first.shape), -turned, turned)


def sibling_rows(one, other):
    left = lane_halves(one.shape)
    half = one.shape[1] // 2
    real = jnp.where(left, one, pltpu.roll(other, half, 1))
    imag = jnp.where(left, pltpu.roll(one, half, 1), other)
    return jnp.concatenate([real, imag], axis=0)


def pairwise(steps, even, odd):
    def step(s, _):
        pl.when(s % 2 == 0)(functools.partial(even, s))
        pl.when(s % 2 == 1)(functools.partial(odd, s))
        return 0

    lax.fori_loop(0, steps, step, 0)


def fetch_order(order_ref, turned, order, order_sem):
    turned[...] = order_ref[...].T
    load = pltpu.make_async_copy(turned, order, order_sem)
    load.start()
    return load


def gather_rows(order, table, segment, held, base):
    for q in range(LANES):
        held[pl.ds(base + q, 1), :] = table[pl.ds(order.at[q][segment], 1), :]


def leaf_kernel(
    first, width, order_ref, ranks_ref, source_ref, basis_hbm, coef_ref,
    table, held0, held1, mixed, basis, turned, order, basis_sem, order_sem,
):
    rhs, _, count = source_ref.shape
    columns = 2 * rhs
    groups, _, points, packed = basis.shape
    segments = points // LANES
    per_group = 4
    load_basis = pltpu.make_async_copy(
        basis_hbm.at[:, pl.ds(first, width)], basis, basis_sem
    )
    load_basis.start()
    load_order = fetch_order(order_ref, turned, order, order_sem)

    def fill(k, _):
        block = pl.ds(pl.multiple_of(k * LANES, LANES), LANES)
        table[block, :columns] = source_ref[:, :, block].reshape(columns, LANES).T.astype(F32)
        return 0

    lax.fori_loop(0, count // LANES, fill, 0, unroll=8)
    load_order.wait()
    load_basis.wait()
    total = groups * width

    def collect(pair, held):
        for part in range(2):
            t = 2 * pair + part
            box = (t // width) * per_group + first + t % width
            for k in range(segments):
                gather_rows(order, table, segments * box + k, held.at[part], k * LANES)

    def project(pair, held):
        for part in range(2):
            t = 2 * pair + part
            group, place = t // width, t % width
            rows = held[part].astype(BF16)[:, :columns]
            mixed[part] = lax.dot_general(
                rows, basis[group, place], (((0,), (0,)), ((), ())), preferred_element_type=F32
            )
            out = packed_sum(
                mixed[part, pl.ds(0, rhs, 2), :], mixed[part, pl.ds(1, rhs, 2), :]
            )
            lane = lax.broadcasted_iota(jnp.int32, out.shape, 1) & (packed // 2 - 1)
            rank = ranks_ref[group * per_group + first + place]
            coef_ref[group, place] = jnp.where(lane < rank, out, 0.0).astype(BF16)

    def even(s):
        project(jnp.maximum(s - 1, 0), held1)
        collect(s, held0)

    def odd(s):
        project(s - 1, held0)
        collect(s, held1)

    pairwise(total // 2, even, odd)
    project(total // 2 - 1, held1)


def leaf_coefs(order, ranks, source, basis, first, width):
    rhs, _, count = source.shape
    groups, _, points, packed = basis.shape
    vmem = pl.BlockSpec(memory_space=pltpu.VMEM)
    smem = pl.BlockSpec(memory_space=pltpu.SMEM)
    hbm = pl.BlockSpec(memory_space=pl.ANY)
    return pl.pallas_call(
        functools.partial(leaf_kernel, first, width),
        out_shape=jax.ShapeDtypeStruct((groups, width, rhs, packed), BF16),
        in_specs=[vmem, smem, vmem, hbm],
        out_specs=vmem,
        scratch_shapes=[
            pltpu.VMEM((count, LANES), F32),
            pltpu.VMEM((2, points, LANES), F32),
            pltpu.VMEM((2, points, LANES), F32),
            pltpu.VMEM((2, 2 * rhs, packed), F32),
            pltpu.VMEM((groups, width, points, packed), BF16),
            pltpu.VMEM((LANES, count // LANES), jnp.int32),
            pltpu.SMEM((LANES, count // LANES), jnp.int32),
            pltpu.SemaphoreType.DMA,
            pltpu.SemaphoreType.DMA,
        ],
        compiler_params=pltpu.CompilerParams(vmem_limit_bytes=24 << 20),
        name="leaf_coefs",
    )(order, ranks, source, basis)


def mix_kernel(level, first, upper_ref, own_ref, other_ref, factor_ref, out_ref):
    groups, width = own_ref.shape[:2]
    upper = upper_ref[0]

    def step(t, _):
        group, place = t // width, t % width
        rows = sibling_rows(own_ref[group, place], other_ref[group, place])
        mine = factor_ref.at[level, group, first + place]
        factor = jnp.concatenate([mine[upper], mine[1 - upper]], axis=0)
        both = jnp.dot(rows, factor, preferred_element_type=F32)
        half = both.shape[0] // 2
        out_ref[group, place] = packed_sum(both[:half], both[half:]).astype(BF16)
        return 0

    lax.fori_loop(0, groups * width, step, 0, unroll=16)


def mix_level(upper, own, other, factors, level, first):
    vmem = pl.BlockSpec(memory_space=pltpu.VMEM)
    return pl.pallas_call(
        functools.partial(mix_kernel, level, first),
        out_shape=jax.ShapeDtypeStruct(own.shape, BF16),
        in_specs=[pl.BlockSpec(memory_space=pltpu.SMEM), vmem, vmem, vmem],
        out_specs=vmem,
        compiler_params=pltpu.CompilerParams(vmem_limit_bytes=16 << 20),
        name="mix_level",
    )(upper, own, other, factors)


def target_kernel(
    order_ref, coef_ref, factor_hbm, basis_hbm, out_ref,
    factor, basis, table, work0, work1, rows, held0, held1, turned, order,
    factor_sem, basis_sem, order_sem,
):
    levels, boxes = factor.shape[:2]
    rhs, packed = coef_ref.shape[1:]
    rank = packed // 2
    points = basis.shape[2] // 2
    columns = 2 * rhs
    blocks = order_ref.shape[0]
    loads = [
        pltpu.make_async_copy(factor_hbm.at[k], factor.at[k], factor_sem.at[k])
        for k in range(levels)
    ]
    loads.append(pltpu.make_async_copy(basis_hbm, basis, basis_sem))
    for load in loads:
        load.start()
    load_order = fetch_order(order_ref, turned, order, order_sem)
    low = 4
    source = coef_ref
    for k in range(levels):
        loads[k].wait()
        sink = (work0, work1)[k % 2]
        stride = low << k

        def pair(p, _, k=k, stride=stride, source=source, sink=sink):
            first = (p // stride) * (2 * stride) + p % stride
            second = first + stride
            lhs = sibling_rows(source[first], source[second])
            for box in (first, second):
                weights = factor[k, box].reshape(packed, packed)
                both = jnp.dot(lhs, weights, preferred_element_type=F32)
                sink[box] = packed_sum(both[:rhs], both[rhs:]).astype(BF16)
            return 0

        lax.fori_loop(0, boxes // 2, pair, 0, unroll=16)
        source = sink
    loads[levels].wait()

    def expand(box, _):
        coef = source[box].astype(F32)
        buf = rows.at[box % 8]
        buf[pl.ds(0, rhs, 2), :] = jnp.where(lane_halves(coef.shape), coef, -coef)
        buf[pl.ds(1, rhs, 2), :] = pltpu.roll(coef, rank, 1)
        weights = basis[box]
        weights = jnp.concatenate([weights[:, :points], weights[:, points:]], axis=0)
        field = jnp.dot(buf[...].astype(BF16), weights, preferred_element_type=F32).astype(BF16)
        spot = pl.ds(pl.multiple_of(box * points, points), points)
        table[spot, :columns] = field.T.astype(F32)
        return 0

    lax.fori_loop(0, boxes, expand, 0, unroll=8)
    load_order.wait()
    many = held0.shape[0]

    def collect(s, held):
        for part in range(many):
            gather_rows(order, table, many * s + part, held.at[part], 0)

    def place(s, held):
        for part in range(many):
            values = held[part].astype(BF16)[:, :columns].T
            spot = pl.ds(pl.multiple_of((many * s + part) * LANES, LANES), LANES)
            out_ref[:, :, spot] = values.reshape(rhs, 2, LANES)

    def even(s):
        place(jnp.maximum(s - 1, 0), held1)
        collect(s, held0)

    def odd(s):
        place(s - 1, held0)
        collect(s, held1)

    pairwise(blocks // many, even, odd)
    place(blocks // many - 1, held1)


def target_fields(order, coef, factors, basis):
    boxes, rhs, packed = coef.shape
    points = basis.shape[2] // 2
    count = boxes * points
    vmem = pl.BlockSpec(memory_space=pltpu.VMEM)
    hbm = pl.BlockSpec(memory_space=pl.ANY)
    return pl.pallas_call(
        target_kernel,
        out_shape=jax.ShapeDtypeStruct((rhs, 2, count), BF16),
        in_specs=[vmem, vmem, hbm, hbm],
        out_specs=vmem,
        scratch_shapes=[
            pltpu.VMEM(factors.shape, BF16),
            pltpu.VMEM(basis.shape, BF16),
            pltpu.VMEM((count, LANES), F32),
            pltpu.VMEM(coef.shape, BF16),
            pltpu.VMEM(coef.shape, BF16),
            pltpu.VMEM((8, 2 * rhs, packed), F32),
            pltpu.VMEM((4, LANES, LANES), F32),
            pltpu.VMEM((4, LANES, LANES), F32),
            pltpu.VMEM((LANES, count // LANES), jnp.int32),
            pltpu.SMEM((LANES, count // LANES), jnp.int32),
            pltpu.SemaphoreType.DMA((factors.shape[0],)),
            pltpu.SemaphoreType.DMA,
            pltpu.SemaphoreType.DMA,
        ],
        compiler_params=pltpu.CompilerParams(vmem_limit_bytes=36 << 20),
        name="target_fields",
    )(order, coef, factors, basis)


def local(
    sources,
    source_order,
    leaf_basis,
    leaf_ranks,
    source_factors,
    target_factors,
    target_basis,
    target_order,
):
    boxes, points, packed = leaf_basis.shape
    rhs, _, count = sources.shape
    groups = lax.axis_size("clu")
    per_group = boxes // groups
    order_in = source_order.reshape(count // LANES, LANES)
    order_out = target_order.reshape(count // LANES, LANES)
    basis = leaf_basis.reshape((groups, per_group) + leaf_basis.shape[1:])
    levels = source_factors.shape[0]
    factors = source_factors.reshape((levels, groups, per_group) + source_factors.shape[2:])
    size = lax.axis_size("lvl")
    uppers = [
        (lax.axis_index("lvl") >> level & 1).reshape(1).astype(jnp.int32)
        for level in range(levels)
    ]
    parts = []
    for first, width in CUTS:
        coef = leaf_coefs(order_in, leaf_ranks, sources, basis, first, width)
        for level in range(levels):
            other = lax.ppermute(coef, "lvl", [(i, i ^ 1 << level) for i in range(size)])
            coef = mix_level(uppers[level], coef, other, factors, level, first)
        parts.append(lax.all_to_all(coef, "clu", split_axis=0, concat_axis=0, tiled=True))
    coef = jnp.concatenate(parts, axis=1).reshape(boxes, rhs, packed)
    return target_fields(order_out, coef, target_factors, target_basis)


def solution(mesh):
    both = ("lvl", "clu")
    placed = (
        P(None, None, both),
        P(both, None),
        P(both, None, None),
        P(both),
        P(None, both, None, None, None),
        P(None, both, None, None, None),
        P(both, None, None),
        P(both, None),
    )
    return jax.shard_map(
        local, mesh=mesh, in_specs=placed, out_specs=P(None, None, both), check_vma=False
    )
```

```python
import functools

import jax
import jax.numpy as jnp
from jax import lax
from jax.experimental import pallas as pl
from jax.experimental.pallas import tpu as pltpu
from jax.sharding import PartitionSpec as P

F32 = jnp.float32
BF16 = jnp.bfloat16
LANES = 128
PER_GROUP = 4
MANY = 8
PARTS = 2
EXTRA = 1
LEAF_LIMIT = 20


def lane_halves(shape):
    return lax.broadcasted_iota(jnp.int32, shape, 1) < shape[1] // 2


def packed_sum(first, second):
    turned = pltpu.roll(second, second.shape[1] // 2, 1)
    return first + jnp.where(lane_halves(first.shape), -turned, turned)


def sibling_rows(one, other):
    left = lane_halves(one.shape)
    half = one.shape[1] // 2
    real = jnp.where(left, one, pltpu.roll(other, half, 1))
    imag = jnp.where(left, pltpu.roll(one, half, 1), other)
    return jnp.concatenate([real, imag], axis=0)


def pairwise(steps, even, odd):
    def step(s, _):
        pl.when(s % 2 == 0)(functools.partial(even, s))
        pl.when(s % 2 == 1)(functools.partial(odd, s))
        return 0

    lax.fori_loop(0, steps, step, 0)


def gather_rows(order, table, segment, held, base):
    for q in range(LANES):
        held[pl.ds(base + q, 1), :] = table[pl.ds(order.at[q][segment], 1), :]


def leaf_boxes(order, ranks_ref, table, basis, coef_refs, held0, held1, mixed, columns):
    groups, width, points, packed = basis.shape
    rhs = columns // 2
    segments = points // LANES
    share = width // len(coef_refs)

    def collect(group, held):
        for place in range(width):
            for k in range(segments):
                segment = segments * (group * width + place) + k
                gather_rows(order, table, segment, held.at[place], k * LANES)

    def project(group, held):
        for place in range(width):
            rows = held[place].astype(BF16)[:, :columns]
            mixed[place] = lax.dot_general(
                rows, basis[group, place], (((0,), (0,)), ((), ())), preferred_element_type=F32
            )
        for place in range(width):
            out = packed_sum(
                mixed[place, pl.ds(0, rhs, 2), :], mixed[place, pl.ds(1, rhs, 2), :]
            )
            lane = lax.broadcasted_iota(jnp.int32, out.shape, 1) & (packed // 2 - 1)
            rank = ranks_ref[group * width + place]
            coef_refs[place // share][group, place % share] = jnp.where(
                lane < rank, out, 0.0
            ).astype(BF16)

    def even(s):
        project(jnp.maximum(s - 1, 0), held1)
        collect(s, held0)

    def odd(s):
        project(s - 1, held0)
        collect(s, held1)

    pairwise(groups, even, odd)
    project(groups - 1, held1)


def leaf_kernel(
    order_hbm, ranks_hbm, source_hbm, basis_hbm, *refs,
):
    loads_hbm, refs = refs[:EXTRA], refs[EXTRA:]
    coef_refs, refs = refs[:PARTS], refs[PARTS:]
    loads_ref, refs = refs[:EXTRA], refs[EXTRA:]
    table, turned, source, basis, held0, held1, mixed, order_vmem, order, ranks, sems = refs
    rhs, _, count = source.shape
    columns = 2 * rhs
    pieces = 4
    cut = count // pieces
    loads = [pltpu.make_async_copy(order_hbm, order_vmem, sems.at[0])]
    for k in range(pieces):
        spot = pl.ds(k * cut, cut)
        loads.append(
            pltpu.make_async_copy(
                source_hbm.at[:, :, spot], source.at[:, :, spot], sems.at[1 + k]
            )
        )
    load_basis = pltpu.make_async_copy(basis_hbm, basis, sems.at[pieces + 1])
    extra = [
        pltpu.make_async_copy(loads_hbm[k].at[0], loads_ref[k], sems.at[pieces + 4 + k])
        for k in range(EXTRA)
    ]
    load_ranks = pltpu.make_async_copy(ranks_hbm, ranks, sems.at[pieces + 2])
    load_order = pltpu.make_async_copy(turned, order, sems.at[pieces + 3])
    for load in loads:
        load.start()
    load_ranks.start()
    load_basis.start()
    for load in extra:
        load.start()
    loads[0].wait()
    turned[...] = order_vmem[...].T
    load_order.start()

    def fill(k, _):
        block = pl.ds(pl.multiple_of(k * LANES, LANES), LANES)
        table[block, :columns] = source[:, :, block].reshape(columns, LANES).T.astype(F32)
        return 0

    blocks = cut // LANES
    for k in range(pieces):
        loads[1 + k].wait()
        lax.fori_loop(k * blocks, (k + 1) * blocks, fill, 0, unroll=8)
    load_order.wait()
    load_ranks.wait()
    load_basis.wait()
    leaf_boxes(order, ranks, table, basis, coef_refs, held0, held1, mixed, columns)
    for load in extra:
        load.wait()


VMEM = pl.BlockSpec(memory_space=pltpu.VMEM)
ANYWHERE = pl.BlockSpec(memory_space=pl.ANY)


def in_hbm(x):
    return pltpu.with_memory_space_constraint(x, pltpu.HBM)


def in_vmem(x):
    return pltpu.with_memory_space_constraint(x, pltpu.VMEM)


def leaf_coefs(order, ranks, source, basis, extra):
    rhs, _, count = source.shape
    groups, width, points, packed = basis.shape
    segments = count // LANES
    coef = jax.ShapeDtypeStruct((groups, width // PARTS, rhs, packed), BF16)
    return pl.pallas_call(
        leaf_kernel,
        out_shape=[coef] * PARTS + [pltpu.VMEM(x.shape[1:], BF16) for x in extra],
        in_specs=[ANYWHERE] * (4 + EXTRA),
        out_specs=[VMEM] * (PARTS + EXTRA),
        scratch_shapes=[
            pltpu.VMEM((count, LANES), F32),
            pltpu.VMEM((LANES, segments), jnp.int32),
            pltpu.VMEM(source.shape, BF16),
            pltpu.VMEM(basis.shape, BF16),
            pltpu.VMEM((width, points, LANES), F32),
            pltpu.VMEM((width, points, LANES), F32),
            pltpu.VMEM((width, 2 * rhs, packed), F32),
            pltpu.VMEM((segments, LANES), jnp.int32),
            pltpu.SMEM((LANES, segments), jnp.int32),
            pltpu.SMEM(ranks.shape, jnp.int32),
            pltpu.SemaphoreType.DMA((8 + EXTRA,)),
        ],
        compiler_params=pltpu.CompilerParams(vmem_limit_bytes=LEAF_LIMIT << 20),
        name="leaf_coefs",
    )(*[in_hbm(x) for x in (order, ranks, source, basis) + tuple(extra)])


def mix_kernel(level, first, resident, upper_ref, own_ref, other_ref, factor_ref, *refs):
    groups, width = own_ref.shape[:2]
    upper = upper_ref[0]
    pieces = 1 if resident else 2
    cut = groups // pieces
    loads = []
    if not resident:
        *refs, factor, sems = refs
        for k in range(pieces):
            spot = pl.ds(k * cut, cut)
            loads.append(
                pltpu.make_async_copy(
                    factor_ref.at[level, spot, pl.ds(first, width)], factor.at[spot], sems.at[k]
                )
            )
        for load in loads:
            load.start()
    out_ref = refs[-1]
    offset = out_ref.shape[1] - width
    if offset:
        out_ref[:, :offset] = refs[0][...]

    def step(t, _):
        group, place = t // width, t % width
        rows = sibling_rows(own_ref[group, place], other_ref[group, place])
        mine = factor_ref.at[group, first + place] if resident else factor.at[group, place]
        weights = jnp.concatenate([mine[upper], mine[1 - upper]], axis=0)
        both = jnp.dot(rows, weights, preferred_element_type=F32)
        half = both.shape[0] // 2
        out_ref[group, offset + place] = packed_sum(both[:half], both[half:]).astype(BF16)
        return 0

    for k in range(pieces):
        if loads:
            loads[k].wait()
        lax.fori_loop(k * cut * width, (k + 1) * cut * width, step, 0, unroll=16)


def mix_level(upper, own, other, factors, level, first, before=(), resident=False):
    groups, width = own.shape[:2]
    full = width + sum(x.shape[1] for x in before)
    scratch = [
        pltpu.VMEM((groups, width) + factors.shape[3:], BF16),
        pltpu.SemaphoreType.DMA((2,)),
    ]
    return pl.pallas_call(
        functools.partial(mix_kernel, level, first, resident),
        out_shape=jax.ShapeDtypeStruct((groups, full) + own.shape[2:], BF16),
        in_specs=[pl.BlockSpec(memory_space=pltpu.SMEM), VMEM, VMEM]
        + [VMEM if resident else ANYWHERE] + [VMEM] * len(before),
        out_specs=VMEM,
        scratch_shapes=[] if resident else scratch,
        compiler_params=pltpu.CompilerParams(vmem_limit_bytes=6 << 20),
        name="mix_level",
    )(upper, own, other, in_vmem(factors) if resident else in_hbm(factors), *before)


def target_kernel(
    order_hbm, coef_ref, factor_hbm, basis_hbm, out_ref,
    factor, basis, table, work0, work1, rows, held0, held1, order_vmem, turned, order, sems,
):
    levels, boxes = factor.shape[:2]
    rhs, packed = coef_ref.shape[1:]
    rank = packed // 2
    points = basis.shape[2] // 2
    columns = 2 * rhs
    blocks = order_vmem.shape[0]
    load = pltpu.make_async_copy(order_hbm, order_vmem, sems.at[0])
    load.start()
    load_order = pltpu.make_async_copy(turned, order, sems.at[1])
    loads = [
        pltpu.make_async_copy(factor_hbm.at[k], factor.at[k], sems.at[2 + k])
        for k in range(levels)
    ]
    loads.append(pltpu.make_async_copy(basis_hbm, basis, sems.at[2 + levels]))
    for item in loads:
        item.start()
    load.wait()
    turned[...] = order_vmem[...].T
    load_order.start()
    low = 4
    source = coef_ref
    for k in range(levels):
        loads[k].wait()
        sink = (work0, work1)[k % 2]
        stride = low << k

        def pair(p, _, k=k, stride=stride, source=source, sink=sink):
            first = (p // stride) * (2 * stride) + p % stride
            second = first + stride
            lhs = sibling_rows(source[first], source[second])
            for box in (first, second):
                weights = factor[k, box].reshape(packed, packed)
                both = jnp.dot(lhs, weights, preferred_element_type=F32)
                sink[box] = packed_sum(both[:rhs], both[rhs:]).astype(BF16)
            return 0

        lax.fori_loop(0, boxes // 2, pair, 0, unroll=32)
        source = sink

    loads[levels].wait()

    def expand(box, _):
        coef = source[box].astype(F32)
        buf = rows.at[box % 16]
        buf[pl.ds(0, rhs, 2), :] = jnp.where(lane_halves(coef.shape), coef, -coef)
        buf[pl.ds(1, rhs, 2), :] = pltpu.roll(coef, rank, 1)
        weights = basis[box]
        weights = jnp.concatenate([weights[:, :points], weights[:, points:]], axis=0)
        field = jnp.dot(buf[...].astype(BF16), weights, preferred_element_type=F32).astype(BF16)
        spot = pl.ds(pl.multiple_of(box * points, points), points)
        table[spot, :columns] = field.T.astype(F32)
        return 0

    lax.fori_loop(0, boxes, expand, 0, unroll=16)
    load_order.wait()
    many = held0.shape[0]

    def collect(s, held):
        for part in range(many):
            gather_rows(order, table, many * s + part, held.at[part], 0)

    def place(s, held):
        for part in range(many):
            values = held[part].astype(BF16)[:, :columns].T
            spot = pl.ds(pl.multiple_of((many * s + part) * LANES, LANES), LANES)
            out_ref[:, :, spot] = values.reshape(rhs, 2, LANES)

    def even(s):
        place(jnp.maximum(s - 1, 0), held1)
        collect(s, held0)

    def odd(s):
        place(s - 1, held0)
        collect(s, held1)

    pairwise(blocks // many, even, odd)
    place(blocks // many - 1, held1)


def target_fields(order, coef, factors, basis):
    boxes, rhs, packed = coef.shape
    points = basis.shape[2] // 2
    count = boxes * points
    return pl.pallas_call(
        target_kernel,
        out_shape=jax.ShapeDtypeStruct((rhs, 2, count), BF16),
        in_specs=[ANYWHERE, VMEM, ANYWHERE, ANYWHERE],
        out_specs=VMEM,
        scratch_shapes=[
            pltpu.VMEM(factors.shape, BF16),
            pltpu.VMEM(basis.shape, BF16),
            pltpu.VMEM((count, LANES), F32),
            pltpu.VMEM(coef.shape, BF16),
            pltpu.VMEM(coef.shape, BF16),
            pltpu.VMEM((16, 2 * rhs, packed), F32),
            pltpu.VMEM((MANY, LANES, LANES), F32),
            pltpu.VMEM((MANY, LANES, LANES), F32),
            pltpu.VMEM((count // LANES, LANES), jnp.int32),
            pltpu.VMEM((LANES, count // LANES), jnp.int32),
            pltpu.SMEM((LANES, count // LANES), jnp.int32),
            pltpu.SemaphoreType.DMA((3 + factors.shape[0],)),
        ],
        compiler_params=pltpu.CompilerParams(vmem_limit_bytes=32 << 20),
        name="target_fields",
    )(in_hbm(order), coef, in_hbm(factors), in_hbm(basis))


def local(
    sources,
    source_order,
    leaf_basis,
    leaf_ranks,
    source_factors,
    target_factors,
    target_basis,
    target_order,
):
    boxes, points, packed = leaf_basis.shape
    rhs, _, count = sources.shape
    groups = lax.axis_size("clu")
    per_group = boxes // groups
    order_in = source_order.reshape(count // LANES, LANES)
    order_out = target_order.reshape(count // LANES, LANES)
    basis = leaf_basis.reshape((groups, per_group) + leaf_basis.shape[1:])
    levels = source_factors.shape[0]
    factors = source_factors.reshape((levels, groups, per_group) + source_factors.shape[2:])
    size = lax.axis_size("lvl")
    uppers = [
        (lax.axis_index("lvl") >> level & 1).reshape(1).astype(jnp.int32)
        for level in range(levels)
    ]
    outs = leaf_coefs(order_in, leaf_ranks, sources, basis, (factors,))
    coefs = list(outs[:PARTS])
    head = outs[PARTS]
    width = per_group // PARTS
    for level in range(levels):
        swap = [(i, i ^ 1 << level) for i in range(size)]
        for k in range(PARTS):
            other = lax.ppermute(coefs[k], "lvl", swap)
            last = level == levels - 1 and k == PARTS - 1
            coefs[k] = mix_level(
                uppers[level], coefs[k], other, factors if level else head, level, k * width,
                coefs[:k] if last else (), level == 0,
            )
    coef = lax.all_to_all(coefs[-1], "clu", split_axis=0, concat_axis=0, tiled=True)
    coef = coef.reshape(boxes, rhs, packed)
    return target_fields(order_out, coef, target_factors, target_basis)


def solution(mesh):
    both = ("lvl", "clu")
    placed = (
        P(None, None, both),
        P(both, None),
        P(both, None, None),
        P(both),
        P(None, both, None, None, None),
        P(None, both, None, None, None),
        P(both, None, None),
        P(both, None),
    )
    return jax.shard_map(
        local, mesh=mesh, in_specs=placed, out_specs=P(None, None, both), check_vma=False
    )
```

```python
import functools

import jax
import jax.numpy as jnp
from jax import lax
from jax.experimental import pallas as pl
from jax.experimental.pallas import tpu as pltpu
from jax.sharding import PartitionSpec as P

F32 = jnp.float32
BF16 = jnp.bfloat16
LANES = 128
PER_GROUP = 4
MANY = 8
PARTS = 2
EXTRA = 1
LEAF_LIMIT = 32
BATCH = 8


def lane_halves(shape):
    return lax.broadcasted_iota(jnp.int32, shape, 1) < shape[1] // 2


def packed_sum(first, second):
    turned = pltpu.roll(second, second.shape[1] // 2, 1)
    return first + jnp.where(lane_halves(first.shape), -turned, turned)


def sibling_rows(one, other):
    left = lane_halves(one.shape)
    half = one.shape[1] // 2
    real = jnp.where(left, one, pltpu.roll(other, half, 1))
    imag = jnp.where(left, pltpu.roll(one, half, 1), other)
    return jnp.concatenate([real, imag], axis=0)


def pairwise(steps, even, odd):
    def step(s, _):
        pl.when(s % 2 == 0)(functools.partial(even, s))
        pl.when(s % 2 == 1)(functools.partial(odd, s))
        return 0

    lax.fori_loop(0, steps, step, 0)


def gather_rows(order, table, segment, held, base):
    for q in range(LANES):
        held[pl.ds(base + q, 1), :] = table[pl.ds(order.at[q][segment], 1), :]


def leaf_boxes(order, ranks_ref, table, basis, coef_refs, held, mixed, columns):
    groups, width, points, packed = basis.shape
    rhs = columns // 2
    segments = points // LANES
    share = width // len(coef_refs)

    def collect(group, _):
        for place in range(width):
            for k in range(segments):
                segment = segments * (group * width + place) + k
                gather_rows(order, table, segment, held.at[group, place], k * LANES)
        return 0

    lax.fori_loop(0, groups, collect, 0)
    lane = lax.broadcasted_iota(jnp.int32, (rhs, packed), 1) & (packed // 2 - 1)

    def project(step, _):
        boxes = [(step * BATCH + g, g, place) for g in range(BATCH) for place in range(width)]
        for group, g, place in boxes:
            rows = held[group, place].astype(BF16)[:, :columns]
            mixed[g, place] = lax.dot_general(
                rows, basis[group, place], (((0,), (0,)), ((), ())), preferred_element_type=F32
            )
        for group, g, place in boxes:
            out = packed_sum(
                mixed[g, place, pl.ds(0, rhs, 2), :], mixed[g, place, pl.ds(1, rhs, 2), :]
            )
            rank = ranks_ref[group * width + place]
            coef_refs[place // share][group, place % share] = jnp.where(
                lane < rank, out, 0.0
            ).astype(BF16)
        return 0

    lax.fori_loop(0, groups // BATCH, project, 0)


def leaf_kernel(
    order_hbm, ranks_hbm, source_hbm, basis_hbm, *refs,
):
    loads_hbm, refs = refs[:EXTRA], refs[EXTRA:]
    coef_refs, refs = refs[:PARTS], refs[PARTS:]
    loads_ref, refs = refs[:EXTRA], refs[EXTRA:]
    table, turned, source, basis, held, mixed, order_vmem, order, ranks, sems = refs
    rhs, _, count = source.shape
    columns = 2 * rhs
    pieces = 4
    cut = count // pieces
    loads = [pltpu.make_async_copy(order_hbm, order_vmem, sems.at[0])]
    for k in range(pieces):
        spot = pl.ds(k * cut, cut)
        loads.append(
            pltpu.make_async_copy(
                source_hbm.at[:, :, spot], source.at[:, :, spot], sems.at[1 + k]
            )
        )
    load_basis = pltpu.make_async_copy(basis_hbm, basis, sems.at[pieces + 1])
    extra = [
        pltpu.make_async_copy(loads_hbm[k].at[0], loads_ref[k], sems.at[pieces + 4 + k])
        for k in range(EXTRA)
    ]
    load_ranks = pltpu.make_async_copy(ranks_hbm, ranks, sems.at[pieces + 2])
    load_order = pltpu.make_async_copy(turned, order, sems.at[pieces + 3])
    for load in loads:
        load.start()
    load_ranks.start()
    load_basis.start()
    for load in extra:
        load.start()
    loads[0].wait()
    turned[...] = order_vmem[...].T
    load_order.start()

    def fill(k, _):
        block = pl.ds(pl.multiple_of(k * LANES, LANES), LANES)
        table[block, :columns] = source[:, :, block].reshape(columns, LANES).T.astype(F32)
        return 0

    blocks = cut // LANES
    for k in range(pieces):
        loads[1 + k].wait()
        lax.fori_loop(k * blocks, (k + 1) * blocks, fill, 0, unroll=8)
    load_order.wait()
    load_ranks.wait()
    load_basis.wait()
    leaf_boxes(order, ranks, table, basis, coef_refs, held, mixed, columns)
    for load in extra:
        load.wait()


VMEM = pl.BlockSpec(memory_space=pltpu.VMEM)
ANYWHERE = pl.BlockSpec(memory_space=pl.ANY)


def in_hbm(x):
    return pltpu.with_memory_space_constraint(x, pltpu.HBM)


def in_vmem(x):
    return pltpu.with_memory_space_constraint(x, pltpu.VMEM)


def leaf_coefs(order, ranks, source, basis, extra):
    rhs, _, count = source.shape
    groups, width, points, packed = basis.shape
    segments = count // LANES
    coef = jax.ShapeDtypeStruct((groups, width // PARTS, rhs, packed), BF16)
    return pl.pallas_call(
        leaf_kernel,
        out_shape=[coef] * PARTS + [pltpu.VMEM(x.shape[1:], BF16) for x in extra],
        in_specs=[ANYWHERE] * (4 + EXTRA),
        out_specs=[VMEM] * (PARTS + EXTRA),
        scratch_shapes=[
            pltpu.VMEM((count, LANES), F32),
            pltpu.VMEM((LANES, segments), jnp.int32),
            pltpu.VMEM(source.shape, BF16),
            pltpu.VMEM(basis.shape, BF16),
            pltpu.VMEM((groups, width, points, LANES), F32),
            pltpu.VMEM((BATCH, width, 2 * rhs, packed), F32),
            pltpu.VMEM((segments, LANES), jnp.int32),
            pltpu.SMEM((LANES, segments), jnp.int32),
            pltpu.SMEM(ranks.shape, jnp.int32),
            pltpu.SemaphoreType.DMA((8 + EXTRA,)),
        ],
        compiler_params=pltpu.CompilerParams(vmem_limit_bytes=LEAF_LIMIT << 20),
        name="leaf_coefs",
    )(*[in_hbm(x) for x in (order, ranks, source, basis) + tuple(extra)])


def mix_kernel(level, first, resident, joined, ahead, upper_ref, own_ref, other_ref, factor_ref, *refs):
    groups, width = own_ref.shape[:2]
    upper = upper_ref[0]
    before, refs = refs[:joined], refs[joined:]
    sources, refs = refs[: len(ahead)], refs[len(ahead) :]
    out_ref, refs = refs[0], refs[1:]
    sinks, refs = refs[: len(ahead)], refs[len(ahead) :]
    *factor, sems = refs
    pieces = 1 if resident else 2
    cut = groups // pieces
    loads = []
    if not resident:
        for k in range(pieces):
            spot = pl.ds(k * cut, cut)
            loads.append(
                pltpu.make_async_copy(
                    factor_ref.at[level, spot, pl.ds(first, width)], factor[0].at[spot], sems.at[k]
                )
            )
    later = [
        pltpu.make_async_copy(
            sources[k].at[row, :, pl.ds(at, size)], sinks[k], sems.at[pieces + k]
        )
        for k, (row, at, size) in enumerate(ahead)
    ]
    for load in loads + later:
        load.start()
    offset = out_ref.shape[1] - width
    if joined:
        out_ref[:, :offset] = before[0][...]

    def step(t, _):
        group, place = t // width, t % width
        rows = sibling_rows(own_ref[group, place], other_ref[group, place])
        mine = factor_ref.at[group, first + place] if resident else factor[0].at[group, place]
        weights = jnp.concatenate([mine[upper], mine[1 - upper]], axis=0)
        both = jnp.dot(rows, weights, preferred_element_type=F32)
        half = both.shape[0] // 2
        out_ref[group, offset + place] = packed_sum(both[:half], both[half:]).astype(BF16)
        return 0

    for k in range(pieces):
        if loads:
            loads[k].wait()
        lax.fori_loop(k * cut * width, (k + 1) * cut * width, step, 0, unroll=cut * width)
    for load in later:
        load.wait()


def mix_level(upper, own, other, factors, level, first, resident=False, before=(), ahead=()):
    groups, width = own.shape[:2]
    full = width + sum(x.shape[1] for x in before)
    scratch = [] if resident else [pltpu.VMEM((groups, width) + factors.shape[3:], BF16)]
    out = jax.ShapeDtypeStruct((groups, full) + own.shape[2:], BF16)
    outs = pl.pallas_call(
        functools.partial(mix_kernel, level, first, resident, len(before), [x[1:] for x in ahead]),
        out_shape=[out] + [pltpu.VMEM((groups, x[3]) + x[0].shape[3:], BF16) for x in ahead],
        in_specs=[pl.BlockSpec(memory_space=pltpu.SMEM), VMEM, VMEM]
        + [VMEM if resident else ANYWHERE]
        + [VMEM] * len(before)
        + [ANYWHERE] * len(ahead),
        out_specs=[VMEM] * (1 + len(ahead)),
        scratch_shapes=scratch + [pltpu.SemaphoreType.DMA((2 + len(ahead),))],
        compiler_params=pltpu.CompilerParams(vmem_limit_bytes=6 << 20),
        name="mix_level",
    )(
        upper, own, other, in_vmem(factors) if resident else in_hbm(factors),
        *before, *[in_hbm(x[0]) for x in ahead],
    )
    return outs[0], list(outs[1:])


def target_levels(coef_ref, head, factor, basis, table, work, rows, loads):
    groups, width, rhs, packed = coef_ref.shape
    points = basis.shape[3] // 2
    columns = 2 * rhs
    source = coef_ref
    for k in range(factor.shape[0] + 1):
        if k:
            loads[k - 1].wait()
        weights_ref = factor.at[k - 1] if k else head
        sink = work.at[k % 2]
        stride = 1 << k

        def pair(p, _, weights_ref=weights_ref, stride=stride, source=source, sink=sink):
            t, place = p // width, p % width
            low = (t // stride) * (2 * stride) + t % stride
            high = low + stride
            lhs = sibling_rows(source[low, place], source[high, place])
            for group in (low, high):
                weights = weights_ref[group, place].reshape(packed, packed)
                both = jnp.dot(lhs, weights, preferred_element_type=F32)
                sink[group, place] = packed_sum(both[:rhs], both[rhs:]).astype(BF16)
            return 0

        lax.fori_loop(0, groups * width // 2, pair, 0, unroll=32)
        source = sink
    loads[-1].wait()

    def expand(t, _):
        group, place = t // width, t % width
        coef = source[group, place].astype(F32)
        buf = rows.at[t % rows.shape[0]]
        buf[pl.ds(0, rhs, 2), :] = jnp.where(lane_halves(coef.shape), coef, -coef)
        buf[pl.ds(1, rhs, 2), :] = pltpu.roll(coef, packed // 2, 1)
        weights = basis[group, place]
        weights = jnp.concatenate([weights[:, :points], weights[:, points:]], axis=0)
        field = jnp.dot(buf[...].astype(BF16), weights, preferred_element_type=F32).astype(BF16)
        table[group, place, :, :columns] = field.T.astype(F32)
        return 0

    lax.fori_loop(0, groups * width, expand, 0, unroll=16)


def target_kernel(
    order_hbm, coef_ref, head, factor_hbm, basis_hbm, out_hbm,
    factor, basis, work, rows, table, held0, held1, order_vmem, turned, order, out, sems, out_sems,
):
    levels = factor.shape[0]
    rhs = coef_ref.shape[2]
    columns = 2 * rhs
    blocks = order_vmem.shape[0]
    load = pltpu.make_async_copy(order_hbm, order_vmem, sems.at[levels + 1])
    load_order = pltpu.make_async_copy(turned, order, sems.at[levels + 2])
    loads = [
        pltpu.make_async_copy(factor_hbm.at[k + 1], factor.at[k], sems.at[k])
        for k in range(levels)
    ]
    loads.append(pltpu.make_async_copy(basis_hbm, basis, sems.at[levels]))
    load.start()
    for item in loads:
        item.start()
    load.wait()
    turned[...] = order_vmem[...].T
    load_order.start()
    target_levels(coef_ref, head, factor, basis, table, work, rows, loads)
    load_order.wait()
    flat = table.reshape(blocks * LANES, LANES)
    many = held0.shape[0]

    def place_part(s, part, held):
        values = held[part].astype(BF16)[:, :columns].T
        spot = pl.ds(pl.multiple_of((many * s + part) * LANES, LANES), LANES)
        out[:, :, spot] = values.reshape(rhs, 2, LANES)

    def both(s, old, new):
        for part in range(many):
            place_part(jnp.maximum(s - 1, 0), part, old)
        for part in range(many):
            gather_rows(order, flat, many * s + part, new.at[part], 0)

    def store(s):
        size = many * LANES
        spot = pl.ds(pl.multiple_of(s * size, size), size)
        return pltpu.make_async_copy(out.at[:, :, spot], out_hbm.at[:, :, spot], out_sems.at[s])

    def even(s):
        both(s, held1, held0)
        pl.when(s > 0)(lambda: store(s - 1).start())

    def odd(s):
        both(s, held0, held1)
        store(s - 1).start()

    steps = blocks // many
    pairwise(steps, even, odd)
    for part in range(many):
        place_part(steps - 1, part, held1)
    store(steps - 1).start()
    for s in range(steps):
        store(s).wait()


def target_fields(order, coef, head, factors, basis):
    groups, width, rhs, packed = coef.shape
    levels, points = factors.shape[0] - 1, basis.shape[3] // 2
    blocks = order.shape[0]
    return pl.pallas_call(
        target_kernel,
        out_shape=jax.ShapeDtypeStruct((rhs, 2, blocks * LANES), BF16),
        in_specs=[ANYWHERE, VMEM, VMEM, ANYWHERE, ANYWHERE],
        out_specs=ANYWHERE,
        scratch_shapes=[
            pltpu.VMEM((levels,) + factors.shape[1:], BF16),
            pltpu.VMEM(basis.shape, BF16),
            pltpu.VMEM((2,) + coef.shape, BF16),
            pltpu.VMEM((16, 2 * rhs, packed), F32),
            pltpu.VMEM((groups, width, points, LANES), F32),
            pltpu.VMEM((MANY, LANES, LANES), F32),
            pltpu.VMEM((MANY, LANES, LANES), F32),
            pltpu.VMEM((blocks, LANES), jnp.int32),
            pltpu.VMEM((LANES, blocks), jnp.int32),
            pltpu.SMEM((LANES, blocks), jnp.int32),
            pltpu.VMEM((rhs, 2, blocks * LANES), BF16),
            pltpu.SemaphoreType.DMA((levels + 3,)),
            pltpu.SemaphoreType.DMA((blocks // MANY,)),
        ],
        compiler_params=pltpu.CompilerParams(vmem_limit_bytes=36 << 20),
        name="target_fields",
    )(in_hbm(order), coef, in_vmem(head), in_hbm(factors), in_hbm(basis))


def local(
    sources,
    source_order,
    leaf_basis,
    leaf_ranks,
    source_factors,
    target_factors,
    target_basis,
    target_order,
):
    boxes, points, packed = leaf_basis.shape
    rhs, _, count = sources.shape
    groups = lax.axis_size("clu")
    per_group = boxes // groups
    order_in = source_order.reshape(count // LANES, LANES)
    order_out = target_order.reshape(count // LANES, LANES)
    basis = leaf_basis.reshape((groups, per_group) + leaf_basis.shape[1:])
    levels = source_factors.shape[0]
    factors = source_factors.reshape((levels, groups, per_group) + source_factors.shape[2:])
    target_w = target_factors.reshape((-1, groups, per_group) + target_factors.shape[2:])
    expansion = target_basis.reshape((groups, per_group) + target_basis.shape[1:])
    size = lax.axis_size("lvl")
    uppers = [
        (lax.axis_index("lvl") >> level & 1).reshape(1).astype(jnp.int32)
        for level in range(levels)
    ]
    outs = leaf_coefs(order_in, leaf_ranks, sources, basis, (factors,))
    coefs = list(outs[:PARTS])
    head = outs[PARTS]
    width = per_group // PARTS
    for level in range(levels):
        swap = [(i, i ^ 1 << level) for i in range(size)]
        last = level == levels - 1
        brought = []
        for k in range(PARTS):
            other = lax.ppermute(coefs[k], "lvl", swap)
            held, at = factors, k * width
            if level == 0:
                held = head
            elif last and k:
                held, at = brought[0], 0
            ahead = ()
            if last and k == 0:
                ahead = ((factors, level, width, per_group - width), (target_w, 0, 0, per_group))
            coefs[k], more = mix_level(
                uppers[level], coefs[k], other, held, level, at,
                resident=held is not factors, before=coefs[:k] if last else (), ahead=ahead,
            )
            brought += more
    coef = lax.all_to_all(coefs[-1], "clu", split_axis=0, concat_axis=0, tiled=True)
    return target_fields(order_out, coef, brought[1], target_w, expansion)


def solution(mesh):
    both = ("lvl", "clu")
    placed = (
        P(None, None, both),
        P(both, None),
        P(both, None, None),
        P(both),
        P(None, both, None, None, None),
        P(None, both, None, None, None),
        P(both, None, None),
        P(both, None),
    )
    return jax.shard_map(
        local, mesh=mesh, in_specs=placed, out_specs=P(None, None, both), check_vma=False
    )
```

```python
import functools

import jax
import jax.numpy as jnp
from jax import lax
from jax.experimental import pallas as pl
from jax.experimental.pallas import tpu as pltpu
from jax.sharding import PartitionSpec as P

F32 = jnp.float32
BF16 = jnp.bfloat16
LANES = 128
PER_GROUP = 4
MANY = 8
PARTS = 2
EXTRA = 1
LEAF_LIMIT = 32
BATCH = 8


def lane_halves(shape):
    return lax.broadcasted_iota(jnp.int32, shape, 1) < shape[1] // 2


def packed_sum(first, second):
    turned = pltpu.roll(second, second.shape[1] // 2, 1)
    return first + jnp.where(lane_halves(first.shape), -turned, turned)


def sibling_rows(one, other):
    left = lane_halves(one.shape)
    half = one.shape[1] // 2
    real = jnp.where(left, one, pltpu.roll(other, half, 1))
    imag = jnp.where(left, pltpu.roll(one, half, 1), other)
    return jnp.concatenate([real, imag], axis=0)


def pairwise(steps, even, odd):
    def step(s, _):
        pl.when(s % 2 == 0)(functools.partial(even, s))
        pl.when(s % 2 == 1)(functools.partial(odd, s))
        return 0

    lax.fori_loop(0, steps, step, 0)


def gather_rows(order, table, segment, held, base):
    for q in range(LANES):
        held[pl.ds(base + q, 1), :] = table[pl.ds(order.at[q][segment], 1), :]


def leaf_boxes(order, ranks_ref, table, basis, coef_refs, held, mixed, columns):
    groups, width, points, packed = basis.shape
    rhs = columns // 2
    segments = points // LANES
    share = width // len(coef_refs)

    def collect(group, _):
        for place in range(width):
            for k in range(segments):
                segment = segments * (group * width + place) + k
                gather_rows(order, table, segment, held.at[group, place], k * LANES)
        return 0

    lax.fori_loop(0, groups, collect, 0)
    lane = lax.broadcasted_iota(jnp.int32, (rhs, packed), 1) & (packed // 2 - 1)

    def project(step, _):
        boxes = [(step * BATCH + g, g, place) for g in range(BATCH) for place in range(width)]
        for group, g, place in boxes:
            rows = held[group, place].astype(BF16)[:, :columns]
            mixed[g, place] = lax.dot_general(
                rows, basis[group, place], (((0,), (0,)), ((), ())), preferred_element_type=F32
            )
        for group, g, place in boxes:
            out = packed_sum(
                mixed[g, place, pl.ds(0, rhs, 2), :], mixed[g, place, pl.ds(1, rhs, 2), :]
            )
            rank = ranks_ref[group * width + place]
            coef_refs[place // share][group, place % share] = jnp.where(
                lane < rank, out, 0.0
            ).astype(BF16)
        return 0

    lax.fori_loop(0, groups // BATCH, project, 0)


def leaf_kernel(
    order_hbm, ranks_hbm, source_hbm, basis_hbm, *refs,
):
    loads_hbm, refs = refs[:EXTRA], refs[EXTRA:]
    coef_refs, refs = refs[:PARTS], refs[PARTS:]
    loads_ref, refs = refs[:EXTRA], refs[EXTRA:]
    table, turned, source, basis, held, mixed, order_vmem, order, ranks, sems = refs
    rhs, _, count = source_hbm.shape
    columns = 2 * rhs
    pieces = 4
    cut = count // pieces
    loads = [pltpu.make_async_copy(order_hbm, order_vmem, sems.at[0])]
    for k in range(pieces):
        spot = pl.ds(k * cut, cut)
        loads.append(
            pltpu.make_async_copy(
                source_hbm.at[:, :, spot], source.at[:, :, spot], sems.at[1 + k]
            )
        )
    load_basis = pltpu.make_async_copy(basis_hbm, basis, sems.at[pieces + 1])
    extra = [
        pltpu.make_async_copy(loads_hbm[k].at[0], loads_ref[k], sems.at[pieces + 4 + k])
        for k in range(EXTRA)
    ]
    load_ranks = pltpu.make_async_copy(ranks_hbm, ranks, sems.at[pieces + 2])
    load_order = pltpu.make_async_copy(turned, order, sems.at[pieces + 3])
    for load in loads:
        load.start()
    load_ranks.start()
    load_basis.start()
    for load in extra:
        load.start()
    loads[0].wait()
    turned[...] = order_vmem[...].T
    load_order.start()

    def fill(k, _):
        block = pl.ds(pl.multiple_of(k * LANES, LANES), LANES)
        table[block, :columns] = source[:, :, block].reshape(columns, LANES).T.astype(F32)
        return 0

    blocks = cut // LANES
    for k in range(pieces):
        loads[1 + k].wait()
        lax.fori_loop(k * blocks, (k + 1) * blocks, fill, 0, unroll=8)
    load_order.wait()
    load_ranks.wait()
    load_basis.wait()
    leaf_boxes(order, ranks, table, basis, coef_refs, held, mixed, columns)
    for load in extra:
        load.wait()


VMEM = pl.BlockSpec(memory_space=pltpu.VMEM)
ANYWHERE = pl.BlockSpec(memory_space=pl.ANY)


def in_hbm(x):
    return pltpu.with_memory_space_constraint(x, pltpu.HBM)


def in_vmem(x):
    return pltpu.with_memory_space_constraint(x, pltpu.VMEM)


def leaf_coefs(order, ranks, source, basis, extra):
    rhs, _, count = source.shape
    groups, width, points, packed = basis.shape
    segments = count // LANES
    coef = jax.ShapeDtypeStruct((groups, width // PARTS, rhs, packed), BF16)
    return pl.pallas_call(
        leaf_kernel,
        out_shape=[coef] * PARTS + [pltpu.VMEM(x.shape[1:], BF16) for x in extra],
        in_specs=[ANYWHERE] * (4 + EXTRA),
        out_specs=[VMEM] * (PARTS + EXTRA),
        scratch_shapes=[
            pltpu.VMEM((count, LANES), F32),
            pltpu.VMEM((LANES, segments), jnp.int32),
            pltpu.VMEM((rhs, 2, count + LANES), BF16),
            pltpu.VMEM(basis.shape, BF16),
            pltpu.VMEM((groups, width, points, LANES), F32),
            pltpu.VMEM((BATCH, width, 2 * rhs, packed), F32),
            pltpu.VMEM((segments, LANES), jnp.int32),
            pltpu.SMEM((LANES, segments), jnp.int32),
            pltpu.SMEM(ranks.shape, jnp.int32),
            pltpu.SemaphoreType.DMA((8 + EXTRA,)),
        ],
        compiler_params=pltpu.CompilerParams(vmem_limit_bytes=LEAF_LIMIT << 20),
        name="leaf_coefs",
    )(*[in_hbm(x) for x in (order, ranks, source, basis) + tuple(extra)])


def mix_kernel(level, first, resident, joined, ahead, upper_ref, own_ref, other_ref, factor_ref, *refs):
    groups, width = own_ref.shape[:2]
    upper = upper_ref[0]
    before, refs = refs[:joined], refs[joined:]
    sources, refs = refs[: len(ahead)], refs[len(ahead) :]
    out_ref, refs = refs[0], refs[1:]
    sinks, refs = refs[: len(ahead)], refs[len(ahead) :]
    *factor, sems = refs
    pieces = 1 if resident else 2
    cut = groups // pieces
    loads = []
    if not resident:
        for k in range(pieces):
            spot = pl.ds(k * cut, cut)
            loads.append(
                pltpu.make_async_copy(
                    factor_ref.at[level, spot, pl.ds(first, width)], factor[0].at[spot], sems.at[k]
                )
            )
    later = [
        pltpu.make_async_copy(
            sources[k].at[row, :, pl.ds(at, size)], sinks[k], sems.at[pieces + k]
        )
        for k, (row, at, size) in enumerate(ahead)
    ]
    for load in loads + later:
        load.start()
    offset = out_ref.shape[1] - width
    if joined:
        out_ref[:, :offset] = before[0][...]

    def step(t, _):
        group, place = t // width, t % width
        rows = sibling_rows(own_ref[group, place], other_ref[group, place])
        mine = factor_ref.at[group, first + place] if resident else factor[0].at[group, place]
        weights = jnp.concatenate([mine[upper], mine[1 - upper]], axis=0)
        both = jnp.dot(rows, weights, preferred_element_type=F32)
        half = both.shape[0] // 2
        out_ref[group, offset + place] = packed_sum(both[:half], both[half:]).astype(BF16)
        return 0

    for k in range(pieces):
        if loads:
            loads[k].wait()
        lax.fori_loop(k * cut * width, (k + 1) * cut * width, step, 0, unroll=cut * width)
    for load in later:
        load.wait()


def mix_level(upper, own, other, factors, level, first, resident=False, before=(), ahead=()):
    groups, width = own.shape[:2]
    full = width + sum(x.shape[1] for x in before)
    scratch = [] if resident else [pltpu.VMEM((groups, width) + factors.shape[3:], BF16)]
    out = jax.ShapeDtypeStruct((groups, full) + own.shape[2:], BF16)
    outs = pl.pallas_call(
        functools.partial(mix_kernel, level, first, resident, len(before), [x[1:] for x in ahead]),
        out_shape=[out] + [pltpu.VMEM((groups, x[3]) + x[0].shape[3:], BF16) for x in ahead],
        in_specs=[pl.BlockSpec(memory_space=pltpu.SMEM), VMEM, VMEM]
        + [VMEM if resident else ANYWHERE]
        + [VMEM] * len(before)
        + [ANYWHERE] * len(ahead),
        out_specs=[VMEM] * (1 + len(ahead)),
        scratch_shapes=scratch + [pltpu.SemaphoreType.DMA((2 + len(ahead),))],
        compiler_params=pltpu.CompilerParams(vmem_limit_bytes=6 << 20),
        name="mix_level",
    )(
        upper, own, other, in_vmem(factors) if resident else in_hbm(factors),
        *before, *[in_hbm(x[0]) for x in ahead],
    )
    return outs[0], list(outs[1:])


def target_levels(coef_ref, head, factor, basis, table, work, rows, loads):
    groups, width, rhs, packed = coef_ref.shape
    points = basis.shape[3] // 2
    columns = 2 * rhs
    source = coef_ref
    for k in range(factor.shape[0] + 1):
        if k:
            loads[k - 1].wait()
        weights_ref = factor.at[k - 1] if k else head
        sink = work.at[k % 2]
        stride = 1 << k

        def pair(p, _, weights_ref=weights_ref, stride=stride, source=source, sink=sink):
            t, place = p // width, p % width
            low = (t // stride) * (2 * stride) + t % stride
            high = low + stride
            lhs = sibling_rows(source[low, place], source[high, place])
            for group in (low, high):
                weights = weights_ref[group, place].reshape(packed, packed)
                both = jnp.dot(lhs, weights, preferred_element_type=F32)
                sink[group, place] = packed_sum(both[:rhs], both[rhs:]).astype(BF16)
            return 0

        lax.fori_loop(0, groups * width // 2, pair, 0, unroll=32)
        source = sink
    loads[-1].wait()

    def expand(t, _):
        group, place = t // width, t % width
        coef = source[group, place].astype(F32)
        buf = rows.at[t % rows.shape[0]]
        buf[pl.ds(0, rhs, 2), :] = jnp.where(lane_halves(coef.shape), coef, -coef)
        buf[pl.ds(1, rhs, 2), :] = pltpu.roll(coef, packed // 2, 1)
        weights = basis[group, place]
        weights = jnp.concatenate([weights[:, :points], weights[:, points:]], axis=0)
        field = jnp.dot(buf[...].astype(BF16), weights, preferred_element_type=F32).astype(BF16)
        table[group, place, :, :columns] = field.T.astype(F32)
        return 0

    lax.fori_loop(0, groups * width, expand, 0, unroll=16)


def target_kernel(
    order_hbm, coef_ref, head, factor_hbm, basis_hbm, out_hbm,
    factor, basis, work, rows, table, held0, held1, order_vmem, turned, order, out, sems, out_sems,
):
    levels = factor.shape[0]
    rhs = coef_ref.shape[2]
    columns = 2 * rhs
    blocks = order_vmem.shape[0]
    load = pltpu.make_async_copy(order_hbm, order_vmem, sems.at[levels + 1])
    load_order = pltpu.make_async_copy(turned, order, sems.at[levels + 2])
    loads = [
        pltpu.make_async_copy(factor_hbm.at[k + 1], factor.at[k], sems.at[k])
        for k in range(levels)
    ]
    loads.append(pltpu.make_async_copy(basis_hbm, basis, sems.at[levels]))
    load.start()
    for item in loads:
        item.start()
    load.wait()
    turned[...] = order_vmem[...].T
    load_order.start()
    target_levels(coef_ref, head, factor, basis, table, work, rows, loads)
    load_order.wait()
    flat = table.reshape(blocks * LANES, LANES)
    many = held0.shape[0]

    def place_part(s, part, held):
        values = held[part].astype(BF16)[:, :columns].T
        spot = pl.ds(pl.multiple_of((many * s + part) * LANES, LANES), LANES)
        out[:, :, spot] = values.reshape(rhs, 2, LANES)

    def both(s, old, new):
        for part in range(many):
            place_part(jnp.maximum(s - 1, 0), part, old)
        for part in range(many):
            gather_rows(order, flat, many * s + part, new.at[part], 0)

    def store(s):
        size = many * LANES
        spot = pl.ds(pl.multiple_of(s * size, size), size)
        return pltpu.make_async_copy(out.at[:, :, spot], out_hbm.at[:, :, spot], out_sems.at[s])

    def even(s):
        both(s, held1, held0)
        pl.when(s > 0)(lambda: store(s - 1).start())

    def odd(s):
        both(s, held0, held1)
        store(s - 1).start()

    steps = blocks // many
    pairwise(steps, even, odd)
    for part in range(many):
        place_part(steps - 1, part, held1)
    store(steps - 1).start()
    for s in range(steps):
        store(s).wait()


def target_fields(order, coef, head, factors, basis):
    groups, width, rhs, packed = coef.shape
    levels, points = factors.shape[0] - 1, basis.shape[3] // 2
    blocks = order.shape[0]
    return pl.pallas_call(
        target_kernel,
        out_shape=jax.ShapeDtypeStruct((rhs, 2, blocks * LANES), BF16),
        in_specs=[ANYWHERE, VMEM, VMEM, ANYWHERE, ANYWHERE],
        out_specs=ANYWHERE,
        scratch_shapes=[
            pltpu.VMEM((levels,) + factors.shape[1:], BF16),
            pltpu.VMEM(basis.shape, BF16),
            pltpu.VMEM((2,) + coef.shape, BF16),
            pltpu.VMEM((16, 2 * rhs, packed), F32),
            pltpu.VMEM((groups, width, points, LANES), F32),
            pltpu.VMEM((MANY, LANES, LANES), F32),
            pltpu.VMEM((MANY, LANES, LANES), F32),
            pltpu.VMEM((blocks, LANES), jnp.int32),
            pltpu.VMEM((LANES, blocks), jnp.int32),
            pltpu.SMEM((LANES, blocks), jnp.int32),
            pltpu.VMEM((rhs, 2, (blocks + 1) * LANES), BF16),
            pltpu.SemaphoreType.DMA((levels + 3,)),
            pltpu.SemaphoreType.DMA((blocks // MANY,)),
        ],
        compiler_params=pltpu.CompilerParams(vmem_limit_bytes=36 << 20),
        name="target_fields",
    )(in_hbm(order), coef, in_vmem(head), in_hbm(factors), in_hbm(basis))


def local(
    sources,
    source_order,
    leaf_basis,
    leaf_ranks,
    source_factors,
    target_factors,
    target_basis,
    target_order,
):
    boxes, points, packed = leaf_basis.shape
    rhs, _, count = sources.shape
    groups = lax.axis_size("clu")
    per_group = boxes // groups
    order_in = source_order.reshape(count // LANES, LANES)
    order_out = target_order.reshape(count // LANES, LANES)
    basis = leaf_basis.reshape((groups, per_group) + leaf_basis.shape[1:])
    levels = source_factors.shape[0]
    factors = source_factors.reshape((levels, groups, per_group) + source_factors.shape[2:])
    target_w = target_factors.reshape((-1, groups, per_group) + target_factors.shape[2:])
    expansion = target_basis.reshape((groups, per_group) + target_basis.shape[1:])
    size = lax.axis_size("lvl")
    uppers = [
        (lax.axis_index("lvl") >> level & 1).reshape(1).astype(jnp.int32)
        for level in range(levels)
    ]
    outs = leaf_coefs(order_in, leaf_ranks, sources, basis, (factors,))
    coefs = list(outs[:PARTS])
    head = outs[PARTS]
    width = per_group // PARTS
    for level in range(levels):
        swap = [(i, i ^ 1 << level) for i in range(size)]
        last = level == levels - 1
        brought = []
        for k in range(PARTS):
            other = lax.ppermute(coefs[k], "lvl", swap)
            held, at = factors, k * width
            if level == 0:
                held = head
            elif level == 1 and k == 0:
                held, at = early[0], 0
            elif last and k:
                held, at = brought[0], 0
            ahead = ()
            if level == 0 and k == PARTS - 1:
                ahead = ((factors, 1, 0, width),)
            if last and k == 0:
                ahead = ((factors, level, width, per_group - width), (target_w, 0, 0, per_group))
            coefs[k], more = mix_level(
                uppers[level], coefs[k], other, held, level, at,
                resident=held is not factors, before=coefs[:k] if last else (), ahead=ahead,
            )
            brought += more
        if level == 0:
            early = brought
    coef = lax.all_to_all(coefs[-1], "clu", split_axis=0, concat_axis=0, tiled=True)
    return target_fields(order_out, coef, brought[1], target_w, expansion)


def solution(mesh):
    both = ("lvl", "clu")
    placed = (
        P(None, None, both),
        P(both, None),
        P(both, None, None),
        P(both),
        P(None, both, None, None, None),
        P(None, both, None, None, None),
        P(both, None, None),
        P(both, None),
    )
    return jax.shard_map(
        local, mesh=mesh, in_specs=placed, out_specs=P(None, None, both), check_vma=False
    )
```

```python
import functools

import jax
import jax.numpy as jnp
from jax import lax
from jax.experimental import pallas as pl
from jax.experimental.pallas import tpu as pltpu
from jax.sharding import PartitionSpec as P

F32 = jnp.float32
BF16 = jnp.bfloat16
LANES = 128
PER_GROUP = 4
MANY = 16
PARTS = 2
EXTRA = 1
LEAF_LIMIT = 32
BATCH = 16


def lane_halves(shape):
    return lax.broadcasted_iota(jnp.int32, shape, 1) < shape[1] // 2


def packed_sum(first, second):
    turned = pltpu.roll(second, second.shape[1] // 2, 1)
    return first + jnp.where(lane_halves(first.shape), -turned, turned)


def sibling_rows(one, other):
    left = lane_halves(one.shape)
    half = one.shape[1] // 2
    real = jnp.where(left, one, pltpu.roll(other, half, 1))
    imag = jnp.where(left, pltpu.roll(one, half, 1), other)
    return jnp.concatenate([real, imag], axis=0)


def pairwise(steps, even, odd):
    def step(s, _):
        pl.when(s % 2 == 0)(functools.partial(even, s))
        pl.when(s % 2 == 1)(functools.partial(odd, s))
        return 0

    lax.fori_loop(0, steps, step, 0)


def gather_rows(order, table, segment, held, base):
    for q in range(LANES):
        held[pl.ds(base + q, 1), :] = table[pl.ds(order.at[q][segment], 1), :]


def leaf_boxes(order, ranks_ref, table, basis, coef_refs, held, mixed, columns):
    groups, width, points, packed = basis.shape
    rhs = columns // 2
    segments = points // LANES
    share = width // len(coef_refs)

    def collect(group, _):
        for place in range(width):
            for k in range(segments):
                segment = segments * (group * width + place) + k
                gather_rows(order, table, segment, held.at[group, place], k * LANES)
        return 0

    lax.fori_loop(0, groups, collect, 0)
    lane = lax.broadcasted_iota(jnp.int32, (rhs, packed), 1) & (packed // 2 - 1)

    def project(step, _):
        boxes = [(step * BATCH + g, g, place) for g in range(BATCH) for place in range(width)]
        for group, g, place in boxes:
            rows = held[group, place].astype(BF16)[:, :columns]
            mixed[g, place] = lax.dot_general(
                rows, basis[group, place], (((0,), (0,)), ((), ())), preferred_element_type=F32
            )
        for group, g, place in boxes:
            out = packed_sum(
                mixed[g, place, pl.ds(0, rhs, 2), :], mixed[g, place, pl.ds(1, rhs, 2), :]
            )
            rank = ranks_ref[group * width + place]
            coef_refs[place // share][group, place % share] = jnp.where(
                lane < rank, out, 0.0
            ).astype(BF16)
        return 0

    lax.fori_loop(0, groups // BATCH, project, 0)


def leaf_kernel(
    order_hbm, ranks_hbm, source_hbm, basis_hbm, *refs,
):
    loads_hbm, refs = refs[:EXTRA], refs[EXTRA:]
    coef_refs, refs = refs[:PARTS], refs[PARTS:]
    loads_ref, refs = refs[:EXTRA], refs[EXTRA:]
    table, turned, source, basis, held, mixed, order_vmem, order, ranks, sems = refs
    rhs, _, count = source_hbm.shape
    columns = 2 * rhs
    pieces = 4
    cut = count // pieces
    loads = [pltpu.make_async_copy(order_hbm, order_vmem, sems.at[0])]
    for k in range(pieces):
        spot = pl.ds(k * cut, cut)
        loads.append(
            pltpu.make_async_copy(
                source_hbm.at[:, :, spot], source.at[:, :, spot], sems.at[1 + k]
            )
        )
    load_basis = pltpu.make_async_copy(basis_hbm, basis, sems.at[pieces + 1])
    extra = [
        pltpu.make_async_copy(loads_hbm[k].at[0], loads_ref[k], sems.at[pieces + 4 + k])
        for k in range(EXTRA)
    ]
    load_ranks = pltpu.make_async_copy(ranks_hbm, ranks, sems.at[pieces + 2])
    load_order = pltpu.make_async_copy(turned, order, sems.at[pieces + 3])
    for load in loads:
        load.start()
    load_ranks.start()
    load_basis.start()
    for load in extra:
        load.start()
    loads[0].wait()
    turned[...] = order_vmem[...].T
    load_order.start()

    def fill(k, _):
        block = pl.ds(pl.multiple_of(k * LANES, LANES), LANES)
        table[block, :columns] = source[:, :, block].reshape(columns, LANES).T.astype(F32)
        return 0

    blocks = cut // LANES
    for k in range(pieces):
        loads[1 + k].wait()
        lax.fori_loop(k * blocks, (k + 1) * blocks, fill, 0, unroll=8)
    load_order.wait()
    load_ranks.wait()
    load_basis.wait()
    leaf_boxes(order, ranks, table, basis, coef_refs, held, mixed, columns)
    for load in extra:
        load.wait()


VMEM = pl.BlockSpec(memory_space=pltpu.VMEM)
ANYWHERE = pl.BlockSpec(memory_space=pl.ANY)


def in_hbm(x):
    return pltpu.with_memory_space_constraint(x, pltpu.HBM)


def in_vmem(x):
    return pltpu.with_memory_space_constraint(x, pltpu.VMEM)


def leaf_coefs(order, ranks, source, basis, extra):
    rhs, _, count = source.shape
    groups, width, points, packed = basis.shape
    segments = count // LANES
    coef = jax.ShapeDtypeStruct((groups, width // PARTS, rhs, packed), BF16)
    return pl.pallas_call(
        leaf_kernel,
        out_shape=[coef] * PARTS + [pltpu.VMEM(x.shape[1:], BF16) for x in extra],
        in_specs=[ANYWHERE] * (4 + EXTRA),
        out_specs=[VMEM] * (PARTS + EXTRA),
        scratch_shapes=[
            pltpu.VMEM((count, LANES), F32),
            pltpu.VMEM((LANES, segments), jnp.int32),
            pltpu.VMEM((rhs, 2, count + LANES), BF16),
            pltpu.VMEM(basis.shape, BF16),
            pltpu.VMEM((groups, width, points, LANES), F32),
            pltpu.VMEM((BATCH, width, 2 * rhs, packed), F32),
            pltpu.VMEM((segments, LANES), jnp.int32),
            pltpu.SMEM((LANES, segments), jnp.int32),
            pltpu.SMEM(ranks.shape, jnp.int32),
            pltpu.SemaphoreType.DMA((8 + EXTRA,)),
        ],
        compiler_params=pltpu.CompilerParams(vmem_limit_bytes=LEAF_LIMIT << 20),
        name="leaf_coefs",
    )(*[in_hbm(x) for x in (order, ranks, source, basis) + tuple(extra)])


def mix_kernel(level, first, resident, joined, ahead, upper_ref, own_ref, other_ref, factor_ref, *refs):
    groups, width = own_ref.shape[:2]
    upper = upper_ref[0]
    before, refs = refs[:joined], refs[joined:]
    sources, refs = refs[: len(ahead)], refs[len(ahead) :]
    out_ref, refs = refs[0], refs[1:]
    sinks, refs = refs[: len(ahead)], refs[len(ahead) :]
    *factor, sems = refs
    pieces = 1 if resident else 2
    cut = groups // pieces
    loads = []
    if not resident:
        for k in range(pieces):
            spot = pl.ds(k * cut, cut)
            loads.append(
                pltpu.make_async_copy(
                    factor_ref.at[level, spot, pl.ds(first, width)], factor[0].at[spot], sems.at[k]
                )
            )
    later = [
        pltpu.make_async_copy(
            sources[k].at[row, :, pl.ds(at, size)], sinks[k], sems.at[pieces + k]
        )
        for k, (row, at, size) in enumerate(ahead)
    ]
    for load in loads + later:
        load.start()
    offset = out_ref.shape[1] - width
    if joined:
        out_ref[:, :offset] = before[0][...]

    def step(t, _):
        group, place = t // width, t % width
        rows = sibling_rows(own_ref[group, place], other_ref[group, place])
        mine = factor_ref.at[group, first + place] if resident else factor[0].at[group, place]
        weights = jnp.concatenate([mine[upper], mine[1 - upper]], axis=0)
        both = jnp.dot(rows, weights, preferred_element_type=F32)
        half = both.shape[0] // 2
        out_ref[group, offset + place] = packed_sum(both[:half], both[half:]).astype(BF16)
        return 0

    for k in range(pieces):
        if loads:
            loads[k].wait()
        lax.fori_loop(k * cut * width, (k + 1) * cut * width, step, 0, unroll=cut * width)
    for load in later:
        load.wait()


def mix_level(upper, own, other, factors, level, first, resident=False, before=(), ahead=()):
    groups, width = own.shape[:2]
    full = width + sum(x.shape[1] for x in before)
    scratch = [] if resident else [pltpu.VMEM((groups, width) + factors.shape[3:], BF16)]
    out = jax.ShapeDtypeStruct((groups, full) + own.shape[2:], BF16)
    outs = pl.pallas_call(
        functools.partial(mix_kernel, level, first, resident, len(before), [x[1:] for x in ahead]),
        out_shape=[out] + [pltpu.VMEM((groups, x[3]) + x[0].shape[3:], BF16) for x in ahead],
        in_specs=[pl.BlockSpec(memory_space=pltpu.SMEM), VMEM, VMEM]
        + [VMEM if resident else ANYWHERE]
        + [VMEM] * len(before)
        + [ANYWHERE] * len(ahead),
        out_specs=[VMEM] * (1 + len(ahead)),
        scratch_shapes=scratch + [pltpu.SemaphoreType.DMA((2 + len(ahead),))],
        compiler_params=pltpu.CompilerParams(vmem_limit_bytes=6 << 20),
        name="mix_level",
    )(
        upper, own, other, in_vmem(factors) if resident else in_hbm(factors),
        *before, *[in_hbm(x[0]) for x in ahead],
    )
    return outs[0], list(outs[1:])


def target_levels(coef_ref, head, factor, basis, table, work, rows, loads):
    groups, width, rhs, packed = coef_ref.shape
    points = basis.shape[3] // 2
    columns = 2 * rhs
    source = coef_ref
    for k in range(factor.shape[0] + 1):
        if k:
            loads[k - 1].wait()
        weights_ref = factor.at[k - 1] if k else head
        sink = work.at[k % 2]
        stride = 1 << k

        def pair(p, _, weights_ref=weights_ref, stride=stride, source=source, sink=sink):
            t, place = p // width, p % width
            low = (t // stride) * (2 * stride) + t % stride
            high = low + stride
            lhs = sibling_rows(source[low, place], source[high, place])
            for group in (low, high):
                weights = weights_ref[group, place].reshape(packed, packed)
                both = jnp.dot(lhs, weights, preferred_element_type=F32)
                sink[group, place] = packed_sum(both[:rhs], both[rhs:]).astype(BF16)
            return 0

        lax.fori_loop(0, groups * width // 2, pair, 0, unroll=32)
        source = sink
    loads[-1].wait()

    def expand(t, _):
        group, place = t // width, t % width
        coef = source[group, place].astype(F32)
        buf = rows.at[t % rows.shape[0]]
        buf[pl.ds(0, rhs, 2), :] = jnp.where(lane_halves(coef.shape), coef, -coef)
        buf[pl.ds(1, rhs, 2), :] = pltpu.roll(coef, packed // 2, 1)
        weights = basis[group, place]
        weights = jnp.concatenate([weights[:, :points], weights[:, points:]], axis=0)
        field = jnp.dot(buf[...].astype(BF16), weights, preferred_element_type=F32).astype(BF16)
        table[group, place, :, :columns] = field.T.astype(F32)
        return 0

    lax.fori_loop(0, groups * width, expand, 0, unroll=16)


def target_kernel(
    order_hbm, coef_ref, head, factor_hbm, basis_hbm, out_hbm,
    factor, basis, work, rows, table, held0, held1, order_vmem, turned, order, out, sems, out_sems,
):
    levels = factor.shape[0]
    rhs = coef_ref.shape[2]
    columns = 2 * rhs
    blocks = order_vmem.shape[0]
    load = pltpu.make_async_copy(order_hbm, order_vmem, sems.at[levels + 1])
    load_order = pltpu.make_async_copy(turned, order, sems.at[levels + 2])
    loads = [
        pltpu.make_async_copy(factor_hbm.at[k + 1], factor.at[k], sems.at[k])
        for k in range(levels)
    ]
    loads.append(pltpu.make_async_copy(basis_hbm, basis, sems.at[levels]))
    load.start()
    for item in loads:
        item.start()
    load.wait()
    turned[...] = order_vmem[...].T
    load_order.start()
    target_levels(coef_ref, head, factor, basis, table, work, rows, loads)
    load_order.wait()
    flat = table.reshape(blocks * LANES, LANES)
    many = held0.shape[0]

    def place_part(s, part, held):
        values = held[part].astype(BF16)[:, :columns].T
        spot = pl.ds(pl.multiple_of((many * s + part) * LANES, LANES), LANES)
        out[:, :, spot] = values.reshape(rhs, 2, LANES)

    def both(s, old, new):
        for part in range(many):
            place_part(jnp.maximum(s - 1, 0), part, old)
        for part in range(many):
            gather_rows(order, flat, many * s + part, new.at[part], 0)

    def store(s):
        size = many * LANES
        spot = pl.ds(pl.multiple_of(s * size, size), size)
        return pltpu.make_async_copy(out.at[:, :, spot], out_hbm.at[:, :, spot], out_sems.at[s])

    def even(s):
        both(s, held1, held0)
        pl.when(s > 0)(lambda: store(s - 1).start())

    def odd(s):
        both(s, held0, held1)
        store(s - 1).start()

    steps = blocks // many
    pairwise(steps, even, odd)
    for part in range(many):
        place_part(steps - 1, part, held1)
    store(steps - 1).start()
    for s in range(steps):
        store(s).wait()


def target_fields(order, coef, head, factors, basis):
    groups, width, rhs, packed = coef.shape
    levels, points = factors.shape[0] - 1, basis.shape[3] // 2
    blocks = order.shape[0]
    return pl.pallas_call(
        target_kernel,
        out_shape=jax.ShapeDtypeStruct((rhs, 2, blocks * LANES), BF16),
        in_specs=[ANYWHERE, VMEM, VMEM, ANYWHERE, ANYWHERE],
        out_specs=ANYWHERE,
        scratch_shapes=[
            pltpu.VMEM((levels,) + factors.shape[1:], BF16),
            pltpu.VMEM(basis.shape, BF16),
            pltpu.VMEM((2,) + coef.shape, BF16),
            pltpu.VMEM((16, 2 * rhs, packed), F32),
            pltpu.VMEM((groups, width, points, LANES), F32),
            pltpu.VMEM((MANY, LANES, LANES), F32),
            pltpu.VMEM((MANY, LANES, LANES), F32),
            pltpu.VMEM((blocks, LANES), jnp.int32),
            pltpu.VMEM((LANES, blocks), jnp.int32),
            pltpu.SMEM((LANES, blocks), jnp.int32),
            pltpu.VMEM((rhs, 2, (blocks + 1) * LANES), BF16),
            pltpu.SemaphoreType.DMA((levels + 3,)),
            pltpu.SemaphoreType.DMA((blocks // MANY,)),
        ],
        compiler_params=pltpu.CompilerParams(vmem_limit_bytes=36 << 20),
        name="target_fields",
    )(in_hbm(order), coef, in_vmem(head), in_hbm(factors), in_hbm(basis))


def local(
    sources,
    source_order,
    leaf_basis,
    leaf_ranks,
    source_factors,
    target_factors,
    target_basis,
    target_order,
):
    boxes, points, packed = leaf_basis.shape
    rhs, _, count = sources.shape
    groups = lax.axis_size("clu")
    per_group = boxes // groups
    order_in = source_order.reshape(count // LANES, LANES)
    order_out = target_order.reshape(count // LANES, LANES)
    basis = leaf_basis.reshape((groups, per_group) + leaf_basis.shape[1:])
    levels = source_factors.shape[0]
    factors = source_factors.reshape((levels, groups, per_group) + source_factors.shape[2:])
    target_w = target_factors.reshape((-1, groups, per_group) + target_factors.shape[2:])
    expansion = target_basis.reshape((groups, per_group) + target_basis.shape[1:])
    size = lax.axis_size("lvl")
    uppers = [
        (lax.axis_index("lvl") >> level & 1).reshape(1).astype(jnp.int32)
        for level in range(levels)
    ]
    outs = leaf_coefs(order_in, leaf_ranks, sources, basis, (factors,))
    coefs = list(outs[:PARTS])
    head = outs[PARTS]
    width = per_group // PARTS
    for level in range(levels):
        swap = [(i, i ^ 1 << level) for i in range(size)]
        last = level == levels - 1
        brought = []
        for k in range(PARTS):
            other = lax.ppermute(coefs[k], "lvl", swap)
            held, at = factors, k * width
            if level == 0:
                held = head
            elif level == 1 and k == 0:
                held, at = early[0], 0
            elif last and k:
                held, at = brought[0], 0
            ahead = ()
            if level == 0 and k == PARTS - 1:
                ahead = ((factors, 1, 0, width),)
            if last and k == 0:
                ahead = ((factors, level, width, per_group - width), (target_w, 0, 0, per_group))
            coefs[k], more = mix_level(
                uppers[level], coefs[k], other, held, level, at,
                resident=held is not factors, before=coefs[:k] if last else (), ahead=ahead,
            )
            brought += more
        if level == 0:
            early = brought
    coef = lax.all_to_all(coefs[-1], "clu", split_axis=0, concat_axis=0, tiled=True)
    return target_fields(order_out, coef, brought[1], target_w, expansion)


def solution(mesh):
    both = ("lvl", "clu")
    placed = (
        P(None, None, both),
        P(both, None),
        P(both, None, None),
        P(both),
        P(None, both, None, None, None),
        P(None, both, None, None, None),
        P(both, None, None),
        P(both, None),
    )
    return jax.shard_map(
        local, mesh=mesh, in_specs=placed, out_specs=P(None, None, both), check_vma=False
    )
```

```python
import functools

import jax
import jax.numpy as jnp
from jax import lax
from jax.experimental import pallas as pl
from jax.experimental.pallas import tpu as pltpu
from jax.sharding import PartitionSpec as P

F32 = jnp.float32
BF16 = jnp.bfloat16
LANES = 128
PER_GROUP = 4
MANY = 8
PARTS = 2
EXTRA = 1
LEAF_LIMIT = 32
BATCH = 8


def lane_halves(shape):
    return lax.broadcasted_iota(jnp.int32, shape, 1) < shape[1] // 2


def packed_sum(first, second):
    turned = pltpu.roll(second, second.shape[1] // 2, 1)
    return first + jnp.where(lane_halves(first.shape), -turned, turned)


def sibling_rows(one, other):
    left = lane_halves(one.shape)
    half = one.shape[1] // 2
    real = jnp.where(left, one, pltpu.roll(other, half, 1))
    imag = jnp.where(left, pltpu.roll(one, half, 1), other)
    return jnp.concatenate([real, imag], axis=0)


def pairwise(steps, even, odd):
    def step(s, _):
        pl.when(s % 2 == 0)(functools.partial(even, s))
        pl.when(s % 2 == 1)(functools.partial(odd, s))
        return 0

    lax.fori_loop(0, steps, step, 0)


def gather_rows(order, table, segment, held, base):
    for q in range(LANES):
        held[pl.ds(base + q, 1), :] = table[pl.ds(order.at[q][segment], 1), :]


def leaf_boxes(order, ranks_ref, table, basis, coef_refs, held, mixed, columns):
    groups, width, points, packed = basis.shape
    rhs = columns // 2
    segments = points // LANES
    share = width // len(coef_refs)

    def collect(group, _):
        for place in range(width):
            for k in range(segments):
                segment = segments * (group * width + place) + k
                gather_rows(order, table, segment, held.at[group, place], k * LANES)
        return 0

    lax.fori_loop(0, groups, collect, 0)
    lane = lax.broadcasted_iota(jnp.int32, (rhs, packed), 1) & (packed // 2 - 1)

    def project(step, _):
        boxes = [(step * BATCH + g, g, place) for g in range(BATCH) for place in range(width)]
        for group, g, place in boxes:
            rows = held[group, place].astype(BF16)[:, :columns]
            mixed[g, place] = lax.dot_general(
                rows, basis[group, place], (((0,), (0,)), ((), ())), preferred_element_type=F32
            )
        for group, g, place in boxes:
            out = packed_sum(
                mixed[g, place, pl.ds(0, rhs, 2), :], mixed[g, place, pl.ds(1, rhs, 2), :]
            )
            rank = ranks_ref[group * width + place]
            coef_refs[place // share][group, place % share] = jnp.where(
                lane < rank, out, 0.0
            ).astype(BF16)
        return 0

    lax.fori_loop(0, groups // BATCH, project, 0)


def leaf_kernel(
    order_hbm, ranks_hbm, source_hbm, basis_hbm, *refs,
):
    loads_hbm, refs = refs[:EXTRA], refs[EXTRA:]
    coef_refs, refs = refs[:PARTS], refs[PARTS:]
    loads_ref, refs = refs[:EXTRA], refs[EXTRA:]
    table, turned, source, basis, held, mixed, order_vmem, order, ranks, sems = refs
    rhs, _, count = source_hbm.shape
    columns = 2 * rhs
    pieces = 4
    cut = count // pieces
    loads = [pltpu.make_async_copy(order_hbm, order_vmem, sems.at[0])]
    for k in range(pieces):
        spot = pl.ds(k * cut, cut)
        loads.append(
            pltpu.make_async_copy(
                source_hbm.at[:, :, spot], source.at[:, :, spot], sems.at[1 + k]
            )
        )
    load_basis = pltpu.make_async_copy(basis_hbm, basis, sems.at[pieces + 1])
    extra = [
        pltpu.make_async_copy(loads_hbm[k].at[0], loads_ref[k], sems.at[pieces + 4 + k])
        for k in range(EXTRA)
    ]
    load_ranks = pltpu.make_async_copy(ranks_hbm, ranks, sems.at[pieces + 2])
    load_order = pltpu.make_async_copy(turned, order, sems.at[pieces + 3])
    for load in loads:
        load.start()
    load_ranks.start()
    load_basis.start()
    for load in extra:
        load.start()
    loads[0].wait()
    turned[...] = order_vmem[...].T
    load_order.start()

    def fill(k, _):
        block = pl.ds(pl.multiple_of(k * LANES, LANES), LANES)
        table[block, :columns] = source[:, :, block].reshape(columns, LANES).T.astype(F32)
        return 0

    blocks = cut // LANES
    for k in range(pieces):
        loads[1 + k].wait()
        lax.fori_loop(k * blocks, (k + 1) * blocks, fill, 0, unroll=8)
    load_order.wait()
    load_ranks.wait()
    load_basis.wait()
    leaf_boxes(order, ranks, table, basis, coef_refs, held, mixed, columns)
    for load in extra:
        load.wait()


VMEM = pl.BlockSpec(memory_space=pltpu.VMEM)
ANYWHERE = pl.BlockSpec(memory_space=pl.ANY)


def in_hbm(x):
    return pltpu.with_memory_space_constraint(x, pltpu.HBM)


def in_vmem(x):
    return pltpu.with_memory_space_constraint(x, pltpu.VMEM)


def leaf_coefs(order, ranks, source, basis, extra):
    rhs, _, count = source.shape
    groups, width, points, packed = basis.shape
    segments = count // LANES
    coef = jax.ShapeDtypeStruct((groups, width // PARTS, rhs, packed), BF16)
    return pl.pallas_call(
        leaf_kernel,
        out_shape=[coef] * PARTS + [pltpu.VMEM(x.shape[1:], BF16) for x in extra],
        in_specs=[ANYWHERE] * (4 + EXTRA),
        out_specs=[VMEM] * (PARTS + EXTRA),
        scratch_shapes=[
            pltpu.VMEM((count, LANES), F32),
            pltpu.VMEM((LANES, segments), jnp.int32),
            pltpu.VMEM((rhs, 2, count + LANES), BF16),
            pltpu.VMEM(basis.shape, BF16),
            pltpu.VMEM((groups, width, points, LANES), F32),
            pltpu.VMEM((BATCH, width, 2 * rhs, packed), F32),
            pltpu.VMEM((segments, LANES), jnp.int32),
            pltpu.SMEM((LANES, segments), jnp.int32),
            pltpu.SMEM(ranks.shape, jnp.int32),
            pltpu.SemaphoreType.DMA((8 + EXTRA,)),
        ],
        compiler_params=pltpu.CompilerParams(vmem_limit_bytes=LEAF_LIMIT << 20),
        name="leaf_coefs",
    )(*[in_hbm(x) for x in (order, ranks, source, basis) + tuple(extra)])


def mix_kernel(level, first, resident, joined, ahead, upper_ref, own_ref, other_ref, factor_ref, *refs):
    groups, width = own_ref.shape[:2]
    upper = upper_ref[0]
    before, refs = refs[:joined], refs[joined:]
    sources, refs = refs[: len(ahead)], refs[len(ahead) :]
    out_ref, refs = refs[0], refs[1:]
    sinks, refs = refs[: len(ahead)], refs[len(ahead) :]
    *factor, sems = refs
    pieces = 1 if resident else 2
    cut = groups // pieces
    loads = []
    if not resident:
        for k in range(pieces):
            spot = pl.ds(k * cut, cut)
            loads.append(
                pltpu.make_async_copy(
                    factor_ref.at[level, spot, pl.ds(first, width)], factor[0].at[spot], sems.at[k]
                )
            )
    later = [
        pltpu.make_async_copy(
            sources[k].at[row, :, pl.ds(at, size)], sinks[k], sems.at[pieces + k]
        )
        for k, (row, at, size) in enumerate(ahead)
    ]
    for load in loads + later:
        load.start()
    offset = out_ref.shape[1] - width
    if joined:
        out_ref[:, :offset] = before[0][...]

    def step(t, _):
        group, place = t // width, t % width
        rows = sibling_rows(own_ref[group, place], other_ref[group, place])
        mine = factor_ref.at[group, first + place] if resident else factor[0].at[group, place]
        weights = jnp.concatenate([mine[upper], mine[1 - upper]], axis=0)
        both = jnp.dot(rows, weights, preferred_element_type=F32)
        half = both.shape[0] // 2
        out_ref[group, offset + place] = packed_sum(both[:half], both[half:]).astype(BF16)
        return 0

    for k in range(pieces):
        if loads:
            loads[k].wait()
        lax.fori_loop(k * cut * width, (k + 1) * cut * width, step, 0, unroll=cut * width)
    for load in later:
        load.wait()


def mix_level(upper, own, other, factors, level, first, resident=False, before=(), ahead=()):
    groups, width = own.shape[:2]
    full = width + sum(x.shape[1] for x in before)
    scratch = [] if resident else [pltpu.VMEM((groups, width) + factors.shape[3:], BF16)]
    out = jax.ShapeDtypeStruct((groups, full) + own.shape[2:], BF16)
    outs = pl.pallas_call(
        functools.partial(mix_kernel, level, first, resident, len(before), [x[1:] for x in ahead]),
        out_shape=[out] + [pltpu.VMEM((groups, x[3]) + x[0].shape[3:], BF16) for x in ahead],
        in_specs=[pl.BlockSpec(memory_space=pltpu.SMEM), VMEM, VMEM]
        + [VMEM if resident else ANYWHERE]
        + [VMEM] * len(before)
        + [ANYWHERE] * len(ahead),
        out_specs=[VMEM] * (1 + len(ahead)),
        scratch_shapes=scratch + [pltpu.SemaphoreType.DMA((2 + len(ahead),))],
        compiler_params=pltpu.CompilerParams(vmem_limit_bytes=3 << 20),
        name="mix_level",
    )(
        upper, own, other, in_vmem(factors) if resident else in_hbm(factors),
        *before, *[in_hbm(x[0]) for x in ahead],
    )
    return outs[0], list(outs[1:])


def target_levels(coef_ref, head, factor, basis, table, work, rows, loads):
    groups, width, rhs, packed = coef_ref.shape
    points = basis.shape[3] // 2
    columns = 2 * rhs
    source = coef_ref
    for k in range(factor.shape[0] + 1):
        if k:
            loads[k - 1].wait()
        weights_ref = factor.at[k - 1] if k else head
        sink = work.at[k % 2]
        stride = 1 << k

        def pair(p, _, weights_ref=weights_ref, stride=stride, source=source, sink=sink):
            t, place = p // width, p % width
            low = (t // stride) * (2 * stride) + t % stride
            high = low + stride
            lhs = sibling_rows(source[low, place], source[high, place])
            for group in (low, high):
                weights = weights_ref[group, place].reshape(packed, packed)
                both = jnp.dot(lhs, weights, preferred_element_type=F32)
                sink[group, place] = packed_sum(both[:rhs], both[rhs:]).astype(BF16)
            return 0

        lax.fori_loop(0, groups * width // 2, pair, 0, unroll=32)
        source = sink
    loads[-1].wait()

    def expand(t, _):
        group, place = t // width, t % width
        coef = source[group, place].astype(F32)
        buf = rows.at[t % rows.shape[0]]
        buf[pl.ds(0, rhs, 2), :] = jnp.where(lane_halves(coef.shape), coef, -coef)
        buf[pl.ds(1, rhs, 2), :] = pltpu.roll(coef, packed // 2, 1)
        weights = basis[group, place]
        weights = jnp.concatenate([weights[:, :points], weights[:, points:]], axis=0)
        field = jnp.dot(buf[...].astype(BF16), weights, preferred_element_type=F32).astype(BF16)
        table[group, place, :, :columns] = field.T.astype(F32)
        return 0

    lax.fori_loop(0, groups * width, expand, 0, unroll=16)


def target_kernel(
    order_hbm, coef_ref, head, factor_hbm, basis_hbm, out_hbm,
    factor, basis, work, rows, table, held0, held1, order_vmem, turned, order, out, sems, out_sems,
):
    levels = factor.shape[0]
    rhs = coef_ref.shape[2]
    columns = 2 * rhs
    blocks = order_vmem.shape[0]
    load = pltpu.make_async_copy(order_hbm, order_vmem, sems.at[levels + 1])
    load_order = pltpu.make_async_copy(turned, order, sems.at[levels + 2])
    loads = [
        pltpu.make_async_copy(factor_hbm.at[k + 1], factor.at[k], sems.at[k])
        for k in range(levels)
    ]
    loads.append(pltpu.make_async_copy(basis_hbm, basis, sems.at[levels]))
    load.start()
    for item in loads:
        item.start()
    load.wait()
    turned[...] = order_vmem[...].T
    load_order.start()
    target_levels(coef_ref, head, factor, basis, table, work, rows, loads)
    load_order.wait()
    flat = table.reshape(blocks * LANES, LANES)
    many = held0.shape[0]

    def place_part(s, part, held):
        values = held[part].astype(BF16)[:, :columns].T
        spot = pl.ds(pl.multiple_of((many * s + part) * LANES, LANES), LANES)
        out[:, :, spot] = values.reshape(rhs, 2, LANES)

    def both(s, old, new):
        for part in range(many):
            place_part(jnp.maximum(s - 1, 0), part, old)
        for part in range(many):
            gather_rows(order, flat, many * s + part, new.at[part], 0)

    def store(s):
        size = many * LANES
        spot = pl.ds(pl.multiple_of(s * size, size), size)
        return pltpu.make_async_copy(out.at[:, :, spot], out_hbm.at[:, :, spot], out_sems.at[s])

    def even(s):
        both(s, held1, held0)
        pl.when(s > 0)(lambda: store(s - 1).start())

    def odd(s):
        both(s, held0, held1)
        store(s - 1).start()

    steps = blocks // many
    pairwise(steps, even, odd)
    for part in range(many):
        place_part(steps - 1, part, held1)
    store(steps - 1).start()
    for s in range(steps):
        store(s).wait()


def target_fields(order, coef, head, factors, basis):
    groups, width, rhs, packed = coef.shape
    levels, points = factors.shape[0] - 1, basis.shape[3] // 2
    blocks = order.shape[0]
    return pl.pallas_call(
        target_kernel,
        out_shape=jax.ShapeDtypeStruct((rhs, 2, blocks * LANES), BF16),
        in_specs=[ANYWHERE, VMEM, VMEM, ANYWHERE, ANYWHERE],
        out_specs=ANYWHERE,
        scratch_shapes=[
            pltpu.VMEM((levels,) + factors.shape[1:], BF16),
            pltpu.VMEM(basis.shape, BF16),
            pltpu.VMEM((2,) + coef.shape, BF16),
            pltpu.VMEM((16, 2 * rhs, packed), F32),
            pltpu.VMEM((groups, width, points, LANES), F32),
            pltpu.VMEM((MANY, LANES, LANES), F32),
            pltpu.VMEM((MANY, LANES, LANES), F32),
            pltpu.VMEM((blocks, LANES), jnp.int32),
            pltpu.VMEM((LANES, blocks), jnp.int32),
            pltpu.SMEM((LANES, blocks), jnp.int32),
            pltpu.VMEM((rhs, 2, (blocks + 1) * LANES), BF16),
            pltpu.SemaphoreType.DMA((levels + 3,)),
            pltpu.SemaphoreType.DMA((blocks // MANY,)),
        ],
        compiler_params=pltpu.CompilerParams(vmem_limit_bytes=36 << 20),
        name="target_fields",
    )(in_hbm(order), coef, in_vmem(head), in_hbm(factors), in_hbm(basis))


def local(
    sources,
    source_order,
    leaf_basis,
    leaf_ranks,
    source_factors,
    target_factors,
    target_basis,
    target_order,
):
    boxes, points, packed = leaf_basis.shape
    rhs, _, count = sources.shape
    groups = lax.axis_size("clu")
    per_group = boxes // groups
    order_in = source_order.reshape(count // LANES, LANES)
    order_out = target_order.reshape(count // LANES, LANES)
    basis = leaf_basis.reshape((groups, per_group) + leaf_basis.shape[1:])
    levels = source_factors.shape[0]
    factors = source_factors.reshape((levels, groups, per_group) + source_factors.shape[2:])
    target_w = target_factors.reshape((-1, groups, per_group) + target_factors.shape[2:])
    expansion = target_basis.reshape((groups, per_group) + target_basis.shape[1:])
    size = lax.axis_size("lvl")
    uppers = [
        (lax.axis_index("lvl") >> level & 1).reshape(1).astype(jnp.int32)
        for level in range(levels)
    ]
    outs = leaf_coefs(order_in, leaf_ranks, sources, basis, (factors,))
    coefs = list(outs[:PARTS])
    head = outs[PARTS]
    width = per_group // PARTS
    for level in range(levels):
        swap = [(i, i ^ 1 << level) for i in range(size)]
        last = level == levels - 1
        brought = []
        for k in range(PARTS):
            other = lax.ppermute(coefs[k], "lvl", swap)
            held, at = factors, k * width
            if level == 0:
                held = head
            elif level == 1 and k == 0:
                held, at = early[0], 0
            elif last and k:
                held, at = brought[0], 0
            ahead = ()
            if level == 0 and k == PARTS - 1:
                ahead = ((factors, 1, 0, width),)
            if last and k == 0:
                ahead = ((factors, level, width, per_group - width), (target_w, 0, 0, per_group))
            coefs[k], more = mix_level(
                uppers[level], coefs[k], other, held, level, at,
                resident=held is not factors, before=coefs[:k] if last else (), ahead=ahead,
            )
            brought += more
        if level == 0:
            early = brought
    coef = lax.all_to_all(coefs[-1], "clu", split_axis=0, concat_axis=0, tiled=True)
    return target_fields(order_out, coef, brought[1], target_w, expansion)


def solution(mesh):
    both = ("lvl", "clu")
    placed = (
        P(None, None, both),
        P(both, None),
        P(both, None, None),
        P(both),
        P(None, both, None, None, None),
        P(None, both, None, None, None),
        P(both, None, None),
        P(both, None),
    )
    return jax.shard_map(
        local, mesh=mesh, in_specs=placed, out_specs=P(None, None, both), check_vma=False
    )
```
